32 devices in a mesh: mem: 4 (over y, x), seqi: 2 (over core), seqo: 4 (over z).
Axes of the slice: x: 2, y: 2, z: 4, core: 2. Of those that a mesh axis runs over, the one named last changes fastest.
Arguments:
- queries: bfloat16 [8, 512, 2048], P(('seqi', 'seqo'), 'mem'), may hold values from -6 to 6
- keys: bfloat16 [8, 512, 2048], P(('seqi', 'seqo'), 'mem'), may hold values from -6 to 6
- values: bfloat16 [8, 512, 2048], P(('seqi', 'seqo'), 'mem'), may hold values from -6 to 6
- log_decay: bfloat16 [16, 8, 512], P(None, ('seqi', 'seqo'), 'mem'), may hold values from -1 to 0
- routes: int32 [8, 512, 2], P(('seqi', 'seqo'), 'mem'), may hold values from 0 to 3, all different within a row; in each aligned block of 128 rows (0 to 127, 128 to 255, ..., all dimensions but the last counted through in order) at most 80 rows name the same one
- route_logits: bfloat16 [8, 512, 2], P(('seqi', 'seqo'), 'mem'), may hold values from -6 to 6
- cotangent: bfloat16 [8, 512, 2048], P(('seqi', 'seqo'), 'mem'), may hold values from -6 to 6
Outputs:
- output: bfloat16 [8, 512, 2048], P(('seqi', 'seqo'), 'mem')
- grad_queries: bfloat16 [8, 512, 2048], P(('seqi', 'seqo'), 'mem')
- grad_keys: bfloat16 [8, 512, 2048], P(('seqi', 'seqo'), 'mem')
- grad_values: bfloat16 [8, 512, 2048], P(('seqi', 'seqo'), 'mem')
The draws below stay inside these ranges and needn't reach their ends.
Inputs may be any that keep to these rules, and one draw needn't show every extreme that they name: `routes`: in the rows of one device no memory is named by more than 80 rows, and in every draw some device names some memory exactly 80 times.
All inputs are finite; a program needn't handle non-finite values.
Results may differ from the reference program's by a relative error of at most 0.014.
Values may be sent and summed in bfloat16 or wider, within the bound.
A program may use at most 448 MiB of HBM per device.

```python
import math
import jax
import jax.numpy as jnp
import numpy as np
from jax import lax

H = 16
DK = 128
SHARD_STEPS = 128
MEMS = 4
CAP = 80
SEGMENT_SPAN = 512
SEGMENT_COUNT = 8
CONTEXT_STEPS = 4096


def draw_log_decay(key, part):
    key = jax.random.fold_in(key, 7)
    storage_channels = jax.random.split(key, 7)
    slow_share = 0.5
    slow = jax.random.uniform(storage_channels[0], (H,)) < slow_share
    slow_rate = jnp.exp(jax.random.uniform(storage_channels[1], (H,), jnp.float32, math.log(0.1), 0.0)) / CONTEXT_STEPS
    fast_rate = jnp.exp(jax.random.uniform(storage_channels[2], (H,), jnp.float32, math.log(1.0 / 50.0), math.log(1.0 / 30.0)))
    forgetting_factors = jnp.where(slow, slow_rate, fast_rate)
    shard_scaling = jnp.exp(jax.random.uniform(storage_channels[3], (H, SEGMENT_COUNT, SEGMENT_SPAN // SHARD_STEPS, 1), jnp.float32, math.log(0.6), math.log(1.5)))
    rough_approximation = jax.random.uniform(storage_channels[4], (H, SEGMENT_COUNT, SEGMENT_SPAN // SHARD_STEPS, SHARD_STEPS), jnp.float32, 0.5, 1.5)
    spike_position_at = jax.random.uniform(storage_channels[5], (1, SEGMENT_COUNT, SEGMENT_SPAN // SHARD_STEPS, SHARD_STEPS)) < 8.0 / CONTEXT_STEPS
    spike_extent = jnp.log(jax.random.uniform(storage_channels[6], (1, SEGMENT_COUNT, SEGMENT_SPAN // SHARD_STEPS, SHARD_STEPS), jnp.float32, 0.5, 0.8))
    module_output_value = -(forgetting_factors[:, None, None, None] * shard_scaling * rough_approximation) + jnp.where(spike_position_at, spike_extent, 0.0)
    return module_output_value.reshape(H, SEGMENT_COUNT, SEGMENT_SPAN).astype(jnp.bfloat16)


def block_scale(key, dims, pieces, low, high):
    loudness = 1.0
    for dim, shards_of in pieces:
        draws = jax.random.uniform(jax.random.fold_in(jax.random.fold_in(key, 6), dim), (shards_of,), jnp.float32, low / len(pieces), high / len(pieces))
        loudness = loudness * jnp.repeat(jnp.exp(draws), dims[dim] // shards_of).reshape((-1,) + (1,) * (len(dims) - 1 - dim))
    return loudness


def deal_out(rng, own, number, rows, number_of, top, bound, skew):
    order = jax.random.permutation(rng, number_of)
    packed, ordinary = shares(number_of, rows * top, bound, skew, True), shares(number_of, rows * top, bound, skew, False)
    places = jnp.arange(number_of)

    def named(sizes, turn):
        used = int((sizes > 0).sum())
        fixed = max(1, used // 4)
        moved = fixed + (places - fixed + turn * (used - fixed)) % max(1, number_of - fixed)
        return jnp.zeros((number_of,), jnp.int32).at[order[jnp.where(places < fixed, places, moved)]].set(jnp.asarray(sizes, jnp.int32))

    sizes = jnp.where(number % 4 == 0, named(packed, number // 4), named(ordinary, number - number // 4 - 1))
    mixed = jax.random.permutation(jax.random.fold_in(own, 3), number_of)
    giver, taker = mixed[0:number_of // 2 * 2:2], mixed[1:number_of // 2 * 2:2]
    margin = jnp.minimum(sizes[giver] - 1, bound - sizes[taker]) // 2
    margin = jnp.where((giver == order[0]) | (taker == order[0]) | (sizes[taker] == 0), 0, jnp.maximum(margin, 0))
    moved = jax.random.randint(jax.random.fold_in(own, 4), (number_of // 2,), 0, 1 << 20) % (margin + 1)
    sizes = sizes.at[giver].add(-moved).at[taker].add(moved)
    members = jnp.searchsorted(jnp.cumsum(sizes), jnp.arange(rows * top), side="right").astype(jnp.int32)
    grid = members.reshape(top, rows).T
    grid = grid[jax.random.permutation(jax.random.fold_in(own, 1), rows)]
    turn = jax.random.randint(jax.random.fold_in(own, 2), (rows, 1), 0, top)
    return jnp.take_along_axis(grid, (jnp.arange(top)[None, :] + turn) % top, axis=1)


def shares(count, total, reach, lean, full):
    portions = [(1 << 20) // math.isqrt(grade ** lean) + 1 for grade in range(1, count + 1)]
    largest = reach if full else min(reach, max(-(-total // count), total * portions[0] // sum(portions)))
    least = 1 if total - largest >= count - 1 else 0
    given, surplus = [largest] + [least] * (count - 1), total - largest - least * (count - 1)
    while surplus > 0:
        candidates = [i for i in range(1, count) if given[i] < largest] or [i for i in range(1, count) if given[i] < reach]
        mass, left = sum([portions[i] for i in candidates]), surplus
        for i in candidates:
            extra = min(reach - given[i], max(1, left * portions[i] // mass), surplus)
            given[i] = given[i] + extra
            surplus = surplus - extra
    return np.array(given)


def noise(own_key, shape, scale, limit, cuts=(), held_as=jnp.bfloat16):
    drawn = jax.random.normal(own_key, shape, jnp.float32) * scale
    if len(cuts) > 0:
        drawn = block_scale(own_key, shape, cuts, -0.22, 0.18) * drawn
    return jnp.clip(drawn, min=-limit, max=limit).astype(held_as)


def setup_inputs(seed: int = 0) -> dict:
    splits = jax.random.split(jax.random.key(seed), 8)
    queries = noise(splits[0], (SEGMENT_COUNT, SEGMENT_SPAN, H * DK), 1.0, 6.0, ((0, 8), (1, 4)))
    keys = noise(splits[1], (SEGMENT_COUNT, SEGMENT_SPAN, H * DK), 1.0, 6.0, ((0, 8), (1, 4)))
    values = noise(splits[2], (SEGMENT_COUNT, SEGMENT_SPAN, H * DK), 1.0, 6.0, ((0, 8), (1, 4)))
    log_decay = draw_log_decay(jax.random.fold_in(splits[7], 71), 0)
    routes_keys = jax.random.split(jax.random.fold_in(splits[4], 1), SEGMENT_COUNT * SEGMENT_SPAN // SHARD_STEPS)
    routes_turns = jax.random.permutation(jax.random.fold_in(splits[4], 3), SEGMENT_COUNT * SEGMENT_SPAN // SHARD_STEPS)
    routes = jax.vmap(lambda own, number: deal_out(jax.random.fold_in(splits[4], 2), own, number, SHARD_STEPS, MEMS, 2, CAP, 2))(routes_keys, routes_turns).reshape((SEGMENT_COUNT, SEGMENT_SPAN, 2))
    route_logits = noise(splits[5], (SEGMENT_COUNT, SEGMENT_SPAN, 2), 1.5, 6.0, ((0, 8), (1, 4)))
    cotangent = noise(splits[6], (SEGMENT_COUNT, SEGMENT_SPAN, H * DK), 1.0, 6.0, ((0, 8), (1, 4)))
    return {"queries": queries, "keys": keys, "values": values, "log_decay": log_decay, "routes": routes, "route_logits": route_logits, "cotangent": cotangent}


HIGH = lax.Precision.HIGHEST

def block_scan(reads, writes, values_in, log_rates):
    span = math.gcd(CONTEXT_STEPS, 256)
    count = CONTEXT_STEPS // span
    lower = jnp.arange(span)[:, None] >= jnp.arange(span)[None, :]

    def shape_blocks(array):
        return array.reshape((count, span) + array.shape[1:])

    def advance(state, block):
        q_block, k_block, v_block, g_block = block
        cumulative = jnp.cumsum(g_block, axis=0)
        spread = cumulative.T[:, :, None] - cumulative.T[:, None, :]
        decay_matrix = jnp.where(lower, jnp.exp(jnp.where(lower, spread, 0.0)), 0.0)
        scores = jnp.einsum('thd,shd->hts', q_block, k_block, precision=HIGH) * decay_matrix
        within = jnp.einsum('hts,she->the', scores, v_block, precision=HIGH)
        carried = jnp.einsum('thd,hde->the', q_block * jnp.exp(cumulative)[:, :, None], state, precision=HIGH)
        tail_decay = jnp.exp(cumulative[-1][None, :] - cumulative)
        updated = jnp.exp(cumulative[-1])[:, None, None] * state + jnp.einsum('shd,she->hde', k_block * tail_decay[:, :, None], v_block, precision=HIGH)
        return (updated, within + carried)
    start = jnp.zeros((H, DK, DK), jnp.float32)
    final_state, outputs = lax.scan(jax.checkpoint(advance), start, (shape_blocks(reads), shape_blocks(writes), shape_blocks(values_in), shape_blocks(log_rates)))
    return outputs.reshape(CONTEXT_STEPS, H, DK)

def rounded(array):
    return lax.optimization_barrier(array.astype(jnp.bfloat16)).astype(jnp.float32)

def reference(queries, keys, values, log_decay, routes, route_logits, cotangent):
    query_all = queries.reshape(CONTEXT_STEPS, H, DK).astype(jnp.float32)
    key_all = keys.reshape(CONTEXT_STEPS, H, DK).astype(jnp.float32)
    value_all = values.reshape(CONTEXT_STEPS, H, DK).astype(jnp.float32)
    cotan_all = cotangent.reshape(CONTEXT_STEPS, H, DK).astype(jnp.float32)
    forgetting_factors = log_decay.reshape(H, CONTEXT_STEPS).T.astype(jnp.float32)
    chosen = routes.reshape(CONTEXT_STEPS, 2)
    logits = route_logits.reshape(CONTEXT_STEPS, 2).astype(jnp.float32)
    first_weight = rounded(jax.nn.sigmoid(logits[:, 0] - logits[:, 1]))
    second_weight = rounded(jax.nn.sigmoid(logits[:, 1] - logits[:, 0]))
    scale = 2.0 / math.sqrt(DK * CONTEXT_STEPS)

    def memory_terms(keep, read_weight):

        def forward(query_in, key_in, value_in):
            return block_scan(query_in * read_weight[:, None, None], key_in * keep[:, None, None], value_in, forgetting_factors * keep[:, None])
        module_output_value, pullback = jax.vjp(forward, query_all, key_all, value_all)
        grads = pullback(cotan_all)
        return [rounded(module_output_value)] + [rounded(item) for item in grads]
    ones = jnp.ones((CONTEXT_STEPS,), jnp.float32)
    totals = memory_terms(ones, ones * scale)
    for memory in range(MEMS):
        hit_first = (chosen[:, 0] == memory).astype(jnp.float32)
        hit_second = (chosen[:, 1] == memory).astype(jnp.float32)
        keep = hit_first + hit_second
        read_weight = (first_weight * hit_first + second_weight * hit_second) * scale
        terms = memory_terms(keep, read_weight)
        totals = [left + right for left, right in zip(totals, terms)]
    shaped = [item.astype(jnp.bfloat16).reshape(SEGMENT_COUNT, SEGMENT_SPAN, H * DK) for item in totals]
    return (shaped[0], shaped[1], shaped[2], shaped[3])
```

```python
import functools
import math

import jax
import jax.numpy as jnp
from jax import lax
from jax.experimental import pallas as pl
from jax.experimental.pallas import tpu as pltpu
from jax.sharding import PartitionSpec as P

DK = 128
MEM_DEV = 1
MESH = pl.DeviceIdType.MESH
F32 = jnp.float32
BF16 = jnp.bfloat16
PAD = 24


def dot(left, right, left_dim, right_dim):
    return lax.dot_general(
        left, right, (((left_dim,), (right_dim,)), ((), ())), preferred_element_type=F32
    )


def tables(gates, chosen, logits, groups, memories, scale):
    heads, span = gates.shape
    held = heads // groups
    first = jax.nn.sigmoid(logits[:, 0] - logits[:, 1]).astype(BF16).astype(F32)
    second = jax.nn.sigmoid(logits[:, 1] - logits[:, 0]).astype(BF16).astype(F32)
    names = jnp.arange(memories, dtype=jnp.int32)[:, None]
    hit_first = (chosen[:, 0][None, :] == names).astype(F32)
    hit_second = (chosen[:, 1][None, :] == names).astype(F32)
    ones = jnp.ones((1, span), F32)
    mask = jnp.concatenate([hit_first + hit_second, ones], 0)
    read = jnp.concatenate([first[None] * hit_first + second[None] * hit_second, ones], 0) * scale
    rates = gates[:, None, :] * mask[None]
    upper = (jnp.arange(span)[:, None] <= jnp.arange(span)[None, :]).astype(F32)
    total = jnp.einsum("het,ts->hes", rates, upper, precision=lax.Precision.HIGHEST)
    middle = total[:, :, span // 2 : span // 2 + 1]
    end = total[:, :, -1:]
    kinds = jnp.stack(
        [
            read[None] * jnp.exp(total - middle),
            read[None] * jnp.exp(total),
            mask[None] * jnp.exp(end - total),
        ],
        1,
    )
    count = memories + 1
    columns = kinds.reshape(groups, held * 3 * count, span).transpose(0, 2, 1)
    columns = jnp.pad(columns, ((0, 0), (0, 0), (0, 128 - held * 3 * count)))
    across = (mask[None] * jnp.exp(middle - total)).reshape(groups, held * count, span)
    decay = jnp.broadcast_to(jnp.exp(end), total.shape).reshape(groups, held * count, span)
    room = ((0, 0), (0, PAD - held * count), (0, 0))
    rows = jnp.concatenate([jnp.pad(across, room), jnp.pad(decay, room)], 1)
    return columns, rows


def kernel(
    groups,
    n_i,
    n_o,
    held,
    count,
    q_ref,
    k_ref,
    v_ref,
    g_ref,
    col_ref,
    row_ref,
    o0_ref,
    o1_ref,
    o2_ref,
    o3_ref,
    x,
    cols,
    rows,
    outs,
    kbs,
    qas,
    local_f,
    local_b,
    run_f,
    run_b,
    enter_f,
    enter_b,
    near_f,
    near_b,
    block_decay,
    derived,
    wire_out,
    wire_in,
    in_send,
    in_recv,
    dec_send,
    dec_recv,
    wire_send,
    wire_recv,
    out_send,
    out_recv,
    own_sem,
):
    span = x.shape[2]
    width = held * DK
    me = lax.axis_index("mem")
    i = lax.axis_index("seqi")
    o = lax.axis_index("seqo")
    inputs = (q_ref, k_ref, v_ref, g_ref)
    outputs = (o0_ref, o1_ref, o2_ref, o3_ref)

    barrier = pltpu.get_barrier_semaphore()
    for off in range(1, groups):
        pl.semaphore_signal(
            barrier, inc=1, device_id={"mem": lax.rem(me + off, groups)}, device_id_type=MESH
        )
    for off in range(1, n_o):
        pl.semaphore_signal(
            barrier, inc=1, device_id={"seqo": lax.rem(o + off, n_o)}, device_id_type=MESH
        )

    @pl.when(i > 0)
    def _():
        pl.semaphore_signal(
            barrier, inc=1, device_id={"seqi": lax.rem(i + n_i - 1, n_i)}, device_id_type=MESH
        )

    @pl.when(i < n_i - 1)
    def _():
        pl.semaphore_signal(
            barrier, inc=1, device_id={"seqi": lax.rem(i + 1, n_i)}, device_id_type=MESH
        )

    sides = jnp.where(i > 0, 1, 0) + jnp.where(i < n_i - 1, 1, 0)
    pl.semaphore_wait(barrier, groups - 1 + n_o - 1 + sides)

    arriving = []
    for off in range(1, groups):
        to = lax.rem(me + off, groups)
        lanes = pl.ds(pl.multiple_of(to * width, width), width)
        pairs = [(ref.at[:, lanes], x.at[a, me]) for a, ref in enumerate(inputs)]
        pairs += [(col_ref.at[to], cols.at[me]), (row_ref.at[to], rows.at[me])]
        for a, (src, dst) in enumerate(pairs):
            copy = pltpu.make_async_remote_copy(
                src_ref=src,
                dst_ref=dst,
                send_sem=in_send.at[off - 1, a],
                recv_sem=in_recv.at[off - 1, a],
                device_id={"mem": to},
                device_id_type=MESH,
            )
            copy.start()
            arriving.append(copy)
    lanes = pl.ds(pl.multiple_of(me * width, width), width)
    pairs = [(ref.at[:, lanes], x.at[a, me]) for a, ref in enumerate(inputs)]
    pairs += [(col_ref.at[me], cols.at[me]), (row_ref.at[me], rows.at[me])]
    own = []
    for a, (src, dst) in enumerate(pairs):
        copy = pltpu.make_async_copy(src, dst, own_sem.at[a])
        copy.start()
        own.append(copy)
    for copy in own:
        copy.wait()
    for copy in arriving:
        copy.wait()

    chunk_decay = [rows[c, PAD:] for c in range(groups)]
    total = jnp.ones((PAD, span), F32)
    for c in range(groups):
        near_f[c] = total
        total = total * chunk_decay[c]
    block_decay[o] = total
    after = jnp.ones((PAD, span), F32)
    for c in reversed(range(groups)):
        near_b[c] = after
        after = after * chunk_decay[c]
    decays = []
    for off in range(1, n_o):
        copy = pltpu.make_async_remote_copy(
            src_ref=block_decay.at[o],
            dst_ref=block_decay.at[o],
            send_sem=dec_send.at[off - 1],
            recv_sem=dec_recv.at[off - 1],
            device_id={"seqo": lax.rem(o + off, n_o)},
            device_id_type=MESH,
        )
        copy.start()
        decays.append(copy)

    run_f[...] = jnp.zeros_like(run_f)
    run_b[...] = jnp.zeros_like(run_b)

    def gather_states(step, carry):
        c = step
        z = groups - 1 - step
        for h in range(held):
            lanes = slice(h * DK, (h + 1) * DK)
            base = h * 3 * count
            col = cols[c]
            key = x[1, c, :, lanes].astype(F32)
            kb = jnp.concatenate(
                [
                    (key * col[:, base + 2 * count + e : base + 2 * count + e + 1]).astype(BF16)
                    for e in range(count)
                ],
                1,
            )
            kbs[c, h] = kb
            state = dot(kb, x[2, c, :, lanes], 0, 0)
            for e in range(count):
                r = slice(e * DK, (e + 1) * DK)
                d = rows[c, PAD + h * count + e : PAD + h * count + e + 1, :]
                old = run_f[h, r, :]
                local_f[c, h, r, :] = old
                run_f[h, r, :] = old * d + state[r]
            col = cols[z]
            query = x[0, z, :, lanes].astype(F32)
            qa = jnp.concatenate(
                [
                    (query * col[:, base + count + e : base + count + e + 1]).astype(BF16)
                    for e in range(count)
                ],
                1,
            )
            qas[z, h] = qa
            state = dot(qa, x[3, z, :, lanes], 0, 0)
            for e in range(count):
                r = slice(e * DK, (e + 1) * DK)
                d = rows[z, PAD + h * count + e : PAD + h * count + e + 1, :]
                old = run_b[h, r, :]
                local_b[z, h, r, :] = old
                run_b[h, r, :] = old * d + state[r]
        return carry

    lax.fori_loop(0, groups, gather_states, 0)

    for copy in decays:
        copy.wait()
    before = jnp.ones((PAD, span), F32)
    later = jnp.ones((PAD, span), F32)
    for b in range(n_o):
        piece = block_decay[b]
        before = before * jnp.where(b < o, piece, 1.0)
        later = later * jnp.where(b > o, piece, 1.0)
    derived[0] = before
    derived[1] = later
    derived[2] = block_decay[o]
    derived[3] = before * later * block_decay[o]

    def scaled(value, kind, h):
        parts = []
        for e in range(count):
            d = derived[kind, h * count + e : h * count + e + 1, :]
            parts.append(value[e * DK : (e + 1) * DK].astype(F32) * d)
        return jnp.concatenate(parts, 0)

    sent = []

    def hop(w, kind, h, axis, to, allowed):
        copy = pltpu.make_async_remote_copy(
            src_ref=wire_out.at[w, kind, h],
            dst_ref=wire_in.at[w, kind, h],
            send_sem=wire_send.at[w, kind, h],
            recv_sem=wire_recv.at[w, kind, h],
            device_id={axis: to},
            device_id_type=MESH,
        )
        pl.when(allowed)(copy.start)
        sent.append((allowed, copy))

    def receive(w, kind, h, present):
        copy = pltpu.make_async_remote_copy(
            src_ref=wire_out.at[w, kind, h],
            dst_ref=wire_in.at[w, kind, h],
            send_sem=wire_send.at[w, kind, h],
            recv_sem=wire_recv.at[w, kind, h],
            device_id={"seqo": lax.rem(o + 1, n_o)},
            device_id_type=MESH,
        )

        @pl.when(present)
        def _():
            copy.wait_recv()

        @pl.when(jnp.logical_not(present))
        def _():
            wire_in[w, kind, h] = jnp.zeros((count * DK, DK), BF16)

    up, down = lax.rem(o + 1, n_o), lax.rem(o + n_o - 1, n_o)
    i_up, i_down = lax.rem(i + 1, n_i), lax.rem(i + n_i - 1, n_i)
    low, high = o > 0, o < n_o - 1
    i_low, i_high = i > 0, i < n_i - 1
    ways = (
        (run_f, low, high, up, down, i_low, i_high, i_up, 0, 1, enter_f),
        (run_b, high, low, down, up, i_high, i_low, i_down, 1, 0, enter_b),
    )

    for h in range(held):
        for w, (run, has_prev, has_next, nxt, prv, _, i_next, _, _, ahead, _) in enumerate(ways):
            receive(w, 0, h, has_prev)
            wire_out[w, 0, h] = (scaled(wire_in[w, 0, h], 2, h) + run[h]).astype(BF16)
            hop(w, 0, h, "seqo", nxt, has_next)
        for w, (run, has_prev, has_next, nxt, prv, _, i_next, _, _, ahead, _) in enumerate(ways):
            receive(w, 1, h, jnp.logical_and(has_next, i_next))
            wire_out[w, 1, h] = (scaled(run[h], ahead, h) + wire_in[w, 1, h].astype(F32)).astype(
                BF16
            )
            hop(w, 1, h, "seqo", prv, jnp.logical_and(has_prev, i_next))
    for h in range(held):
        for w, (run, _, _, _, _, i_prev, i_next, i_nxt, behind, ahead, enter) in enumerate(ways):
            receive(w, 2, h, i_prev)
            group = scaled(scaled(wire_in[w, 0, h], 2, h), ahead, h) + wire_out[w, 1, h].astype(F32)
            wire_out[w, 2, h] = (scaled(wire_in[w, 2, h], 3, h) + group).astype(BF16)
            hop(w, 2, h, "seqi", i_nxt, i_next)
            enter[h] = scaled(wire_in[w, 2, h], behind, h) + wire_in[w, 0, h].astype(F32)

    lower = lax.broadcasted_iota(jnp.int32, (span, span), 0) >= lax.broadcasted_iota(
        jnp.int32, (span, span), 1
    )

    def leaving(step, a):
        to = lax.rem(me + 1 + step, groups)
        lanes = pl.ds(pl.multiple_of(me * width, width), width)
        return pltpu.make_async_remote_copy(
            src_ref=outs.at[a, to],
            dst_ref=outputs[a].at[:, lanes],
            send_sem=out_send.at[step, a],
            recv_sem=out_recv.at[step, a],
            device_id={"mem": to},
            device_id_type=MESH,
        )

    def finish(step, carry):
        c = lax.rem(me + 1 + step, groups)
        col = cols[c]
        for h in range(held):
            lanes = slice(h * DK, (h + 1) * DK)
            base = h * 3 * count
            q, k, v, g = (x[a, c, :, lanes] for a in range(4))
            weight = jnp.zeros((span, span), F32)
            for e in range(count):
                j = h * count + e
                weight += col[:, base + e : base + e + 1] * rows[c, j : j + 1, :]
            weight = jnp.where(lower, weight, 0.0)
            sw = (dot(q, k, 1, 1) * weight).astype(BF16)
            gw = (dot(g, v, 1, 1) * weight).astype(BF16)
            past, future = [], []
            for e in range(count):
                j = h * count + e
                r = slice(e * DK, (e + 1) * DK)
                past.append(
                    (local_f[c, h, r, :] + enter_f[h, r, :] * near_f[c, j : j + 1, :]).astype(BF16)
                )
                future.append(
                    (local_b[c, h, r, :] + enter_b[h, r, :] * near_b[c, j : j + 1, :]).astype(BF16)
                )
            past = jnp.concatenate(past, 0)
            future = jnp.concatenate(future, 0)
            out = dot(sw, v, 1, 0) + dot(qas[c, h], past, 1, 0)
            grad_v = dot(sw, g, 0, 0) + dot(kbs[c, h], future, 1, 0)
            grad_q = dot(gw, k, 1, 0)
            grad_k = dot(gw, q, 0, 0)
            from_past = dot(g, past, 1, 1)
            from_future = dot(v, future, 1, 1)
            for e in range(count):
                r = slice(e * DK, (e + 1) * DK)
                ra = base + count + e
                rb = base + 2 * count + e
                grad_q += from_past[:, r] * col[:, ra : ra + 1]
                grad_k += from_future[:, r] * col[:, rb : rb + 1]
            for a, value in enumerate((out, grad_q, grad_k, grad_v)):
                outs[a, c, :, lanes] = value.astype(BF16)

        @pl.when(step < groups - 1)
        def _():
            for a in range(4):
                leaving(step, a).start()

        return carry

    lax.fori_loop(0, groups, finish, 0)
    lanes = pl.ds(pl.multiple_of(me * width, width), width)
    own = []
    for a in range(4):
        copy = pltpu.make_async_copy(outs.at[a, me], outputs[a].at[:, lanes], own_sem.at[a])
        copy.start()
        own.append(copy)
    for copy in own:
        copy.wait()
    for allowed, copy in sent:
        pl.when(allowed)(copy.wait_send)
    for step in range(groups - 1):
        for a in range(4):
            leaving(step, a).wait()


def body(queries, keys, values, log_decay, routes, route_logits, cotangent):
    groups = lax.axis_size("mem")
    n_i = lax.axis_size("seqi")
    n_o = lax.axis_size("seqo")
    memories = MEM_DEV * groups
    span, features = queries.shape[1:]
    heads = log_decay.shape[0]
    held = heads // groups
    count = memories + 1
    scale = 2.0 / math.sqrt(DK * span * groups * n_i * n_o)
    columns, rows = tables(
        log_decay[:, 0, :].astype(F32),
        routes[0],
        route_logits[0].astype(F32),
        groups,
        memories,
        scale,
    )
    any_spec = pl.BlockSpec(memory_space=pl.ANY)
    state = (held, count * DK, DK)
    result = jax.ShapeDtypeStruct((span, features), BF16)
    dma = pltpu.SemaphoreType.DMA
    results = pl.pallas_call(
        functools.partial(kernel, groups, n_i, n_o, held, count),
        out_shape=[result] * 4,
        in_specs=[any_spec] * 6,
        out_specs=[any_spec] * 4,
        scratch_shapes=[
            pltpu.VMEM((4, groups, span, held * DK), BF16),
            pltpu.VMEM((groups, span, 128), F32),
            pltpu.VMEM((groups, 2 * PAD, span), F32),
            pltpu.VMEM((4, groups, span, held * DK), BF16),
            pltpu.VMEM((groups, held, span, count * DK), BF16),
            pltpu.VMEM((groups, held, span, count * DK), BF16),
            pltpu.VMEM((groups,) + state, F32),
            pltpu.VMEM((groups,) + state, F32),
            pltpu.VMEM(state, F32),
            pltpu.VMEM(state, F32),
            pltpu.VMEM(state, F32),
            pltpu.VMEM(state, F32),
            pltpu.VMEM((groups, PAD, span), F32),
            pltpu.VMEM((groups, PAD, span), F32),
            pltpu.VMEM((n_o, PAD, span), F32),
            pltpu.VMEM((4, PAD, span), F32),
            pltpu.VMEM((2, 3) + state, BF16),
            pltpu.VMEM((2, 3) + state, BF16),
            dma((groups - 1, 6)),
            dma((groups - 1, 6)),
            dma((n_o - 1,)),
            dma((n_o - 1,)),
            dma((2, 3, held)),
            dma((2, 3, held)),
            dma((groups - 1, 4)),
            dma((groups - 1, 4)),
            dma((6,)),
        ],
        compiler_params=pltpu.CompilerParams(
            collective_id=0, has_side_effects=True, vmem_limit_bytes=56 * 1024 * 1024
        ),
        cost_estimate=pl.CostEstimate(
            flops=2 * 36 * heads * DK * DK * span,
            bytes_accessed=16 * span * features,
            transcendentals=0,
        ),
    )(queries[0], keys[0], values[0], cotangent[0], columns, rows)
    return tuple(item[None] for item in results)


def solution(mesh):
    rows = P(("seqi", "seqo"), "mem", None)
    return jax.shard_map(
        body,
        mesh=mesh,
        in_specs=(rows, rows, rows, P(None, ("seqi", "seqo"), "mem"), rows, rows, rows),
        out_specs=(rows, rows, rows, rows),
        check_vma=False,
    )
```

```python
import functools
import math

import jax
import jax.numpy as jnp
from jax import lax
from jax.experimental import pallas as pl
from jax.experimental.pallas import tpu as pltpu
from jax.sharding import PartitionSpec as P

DK = 128
MEM_DEV = 1
MESH = pl.DeviceIdType.MESH
F32 = jnp.float32
BF16 = jnp.bfloat16


def dot(left, right, left_dim, right_dim):
    return lax.dot_general(
        left, right, (((left_dim,), (right_dim,)), ((), ())), preferred_element_type=F32
    )


def tables(gates, chosen, logits, groups, memories, scale):
    heads, span = gates.shape
    held = heads // groups
    first = jax.nn.sigmoid(logits[:, 0] - logits[:, 1]).astype(BF16).astype(F32)
    second = jax.nn.sigmoid(logits[:, 1] - logits[:, 0]).astype(BF16).astype(F32)
    names = jnp.arange(memories, dtype=jnp.int32)[:, None]
    hit_first = (chosen[:, 0][None, :] == names).astype(F32)
    hit_second = (chosen[:, 1][None, :] == names).astype(F32)
    ones = jnp.ones((1, span), F32)
    mask = jnp.concatenate([hit_first + hit_second, ones], 0)
    read = jnp.concatenate([first[None] * hit_first + second[None] * hit_second, ones], 0) * scale
    rates = gates[:, None, :] * mask[None]
    upper = (jnp.arange(span)[:, None] <= jnp.arange(span)[None, :]).astype(F32)
    total = jnp.einsum("het,ts->hes", rates, upper, precision=lax.Precision.HIGHEST)
    middle = total[:, :, span // 2 : span // 2 + 1]
    end = total[:, :, -1:]
    count = memories + 1
    kinds = jnp.concatenate(
        [
            read[None] * jnp.exp(total - middle),
            read[None] * jnp.exp(total),
            mask[None] * jnp.exp(end - total),
            jnp.zeros((heads, 16 - 3 * count, span), F32),
            mask[None] * jnp.exp(middle - total),
            jnp.zeros((heads, 8 - count, span), F32),
            jnp.broadcast_to(jnp.exp(end), total.shape),
            jnp.zeros((heads, 8 - count, span), F32),
        ],
        1,
    )
    return kinds.reshape(groups, held, 32, span)


def kernel(
    groups,
    n_i,
    n_o,
    held,
    count,
    q_ref,
    k_ref,
    v_ref,
    g_ref,
    row_ref,
    o0_ref,
    o1_ref,
    o2_ref,
    o3_ref,
    x,
    rows,
    cols,
    outs,
    part,
    kbs,
    qas,
    local_f,
    local_b,
    run_f,
    run_b,
    enter_f,
    enter_b,
    near_f,
    near_b,
    block_decay,
    derived,
    wire_out,
    wire_in,
    row_send,
    row_recv,
    in_send,
    in_recv,
    dec_send,
    dec_recv,
    wire_send,
    wire_recv,
    out_send,
    out_recv,
    row_sem,
    own_sem,
):
    span = x.shape[3]
    width = held * DK
    me = lax.axis_index("mem")
    i = lax.axis_index("seqi")
    o = lax.axis_index("seqo")
    inputs = (q_ref, k_ref, v_ref, g_ref)
    outputs = (o0_ref, o1_ref, o2_ref, o3_ref)

    barrier = pltpu.get_barrier_semaphore()
    for off in range(1, groups):
        pl.semaphore_signal(
            barrier, inc=1, device_id={"mem": lax.rem(me + off, groups)}, device_id_type=MESH
        )
    for off in range(1, n_o):
        pl.semaphore_signal(
            barrier, inc=1, device_id={"seqo": lax.rem(o + off, n_o)}, device_id_type=MESH
        )

    @pl.when(i > 0)
    def _():
        pl.semaphore_signal(
            barrier, inc=1, device_id={"seqi": lax.rem(i + n_i - 1, n_i)}, device_id_type=MESH
        )

    @pl.when(i < n_i - 1)
    def _():
        pl.semaphore_signal(
            barrier, inc=1, device_id={"seqi": lax.rem(i + 1, n_i)}, device_id_type=MESH
        )

    sides = jnp.where(i > 0, 1, 0) + jnp.where(i < n_i - 1, 1, 0)
    pl.semaphore_wait(barrier, groups - 1 + n_o - 1 + sides)

    def row_copy(off):
        to = lax.rem(me + off, groups)
        return pltpu.make_async_remote_copy(
            src_ref=row_ref.at[to],
            dst_ref=rows.at[me],
            send_sem=row_send.at[off - 1],
            recv_sem=row_recv.at[off - 1],
            device_id={"mem": to},
            device_id_type=MESH,
        )

    def in_copy(off, h, a):
        to = lax.rem(me + off, groups)
        lanes = pl.ds(pl.multiple_of((to * held + h) * DK, DK), DK)
        return pltpu.make_async_remote_copy(
            src_ref=inputs[a].at[:, lanes],
            dst_ref=x.at[a, h, me],
            send_sem=in_send.at[off - 1, h, a],
            recv_sem=in_recv.at[off - 1, h, a],
            device_id={"mem": to},
            device_id_type=MESH,
        )

    def own_copy(h, a):
        lanes = pl.ds(pl.multiple_of((me * held + h) * DK, DK), DK)
        return pltpu.make_async_copy(inputs[a].at[:, lanes], x.at[a, h, me], own_sem.at[h, a])

    for off in range(1, groups):
        row_copy(off).start()
    own_rows = pltpu.make_async_copy(row_ref.at[me], rows.at[me], row_sem)
    own_rows.start()

    def start_in(h, carry):
        for a in range(4):
            for off in range(1, groups):
                in_copy(off, h, a).start()
            own_copy(h, a).start()
        return carry

    lax.fori_loop(0, held, start_in, 0)
    own_rows.wait()
    for off in range(1, groups):
        row_copy(off).wait()

    chunk_decay = [rows[c, :, 24:32, :] for c in range(groups)]
    total = jnp.ones((held, 8, span), F32)
    for c in range(groups):
        near_f[c] = total
        total = total * chunk_decay[c]
    block_decay[o] = total
    after = jnp.ones((held, 8, span), F32)
    for c in reversed(range(groups)):
        near_b[c] = after
        after = after * chunk_decay[c]
    decays = []
    for off in range(1, n_o):
        copy = pltpu.make_async_remote_copy(
            src_ref=block_decay.at[o],
            dst_ref=block_decay.at[o],
            send_sem=dec_send.at[off - 1],
            recv_sem=dec_recv.at[off - 1],
            device_id={"seqo": lax.rem(o + off, n_o)},
            device_id_type=MESH,
        )
        copy.start()
        decays.append(copy)

    def block(e):
        return slice(e * DK, (e + 1) * DK)

    def gather_states(h):
        run_f[h] = jnp.zeros((DK, count * DK), F32)
        run_b[h] = jnp.zeros((DK, count * DK), F32)
        for c in range(groups):
            col = rows[c, h, 0:16, :].T
            cols[c, h] = col
            for a, saved, first in ((1, kbs, 2 * count), (0, qas, count)):
                value = x[a, h, c].astype(F32)
                saved[c, h] = jnp.concatenate(
                    [
                        (value * col[:, first + e : first + e + 1]).astype(BF16)
                        for e in range(count)
                    ],
                    1,
                )
        for step in range(groups):
            for c, a, saved, run, local in (
                (step, 2, kbs, run_f, local_f),
                (groups - 1 - step, 3, qas, run_b, local_b),
            ):
                state = dot(x[a, h, c], saved[c, h], 0, 0)
                for e in range(count):
                    old = run[h, :, block(e)]
                    local[c, h, :, block(e)] = old
                    run[h, :, block(e)] = old * rows[c, h, 24 + e : 25 + e, :] + state[:, block(e)]

    lower = lax.broadcasted_iota(jnp.int32, (span, span), 0) >= lax.broadcasted_iota(
        jnp.int32, (span, span), 1
    )

    def within(h):
        for c in range(groups):
            q, k, v, g = (x[a, h, c] for a in range(4))
            col = cols[c, h]
            weight = jnp.zeros((span, span), F32)
            for e in range(count):
                weight += col[:, e : e + 1] * rows[c, h, 16 + e : 17 + e, :]
            weight = jnp.where(lower, weight, 0.0)
            sw = (dot(q, k, 1, 1) * weight).astype(BF16)
            gw = (dot(g, v, 1, 1) * weight).astype(BF16)
            part[0, c, h] = dot(sw, v, 1, 0)
            part[1, c, h] = dot(gw, k, 1, 0)
            part[2, c, h] = dot(gw, q, 0, 0)
            part[3, c, h] = dot(sw, g, 0, 0)

    def scaled(value, kind, h):
        return jnp.concatenate(
            [
                value[:, block(e)].astype(F32) * derived[kind, h, e : e + 1, :]
                for e in range(count)
            ],
            1,
        )

    def hop(w, kind, h, axis, to):
        return pltpu.make_async_remote_copy(
            src_ref=wire_out.at[w, kind, h],
            dst_ref=wire_in.at[w, kind, h],
            send_sem=wire_send.at[w, kind, h],
            recv_sem=wire_recv.at[w, kind, h],
            device_id={axis: to},
            device_id_type=MESH,
        )

    up, down = lax.rem(o + 1, n_o), lax.rem(o + n_o - 1, n_o)
    i_up, i_down = lax.rem(i + 1, n_i), lax.rem(i + n_i - 1, n_i)
    low, high = o > 0, o < n_o - 1
    i_low, i_high = i > 0, i < n_i - 1
    runs = (run_f, run_b)
    enters = (enter_f, enter_b)
    along = ((low, high, up), (high, low, down))
    across = ((i_low, i_high, i_up), (i_high, i_low, i_down))
    links = []
    for w in range(2):
        links.append((w, 0, "seqo") + along[w])
        has, to_has, to = along[1 - w]
        passes = across[w][1]
        links.append(
            (w, 1, "seqo", jnp.logical_and(has, passes), jnp.logical_and(to_has, passes), to)
        )
        links.append((w, 2, "seqi") + across[w])
    links = {(w, kind): rest for w, kind, *rest in links}

    def receive(w, kind, h):
        axis, present, _, to = links[w, kind]

        @pl.when(present)
        def _():
            hop(w, kind, h, axis, to).wait_recv()

        @pl.when(jnp.logical_not(present))
        def _():
            wire_in[w, kind, h] = jnp.zeros((DK, count * DK), BF16)

    def send(w, kind, h):
        axis, _, allowed, to = links[w, kind]

        @pl.when(allowed)
        def _():
            hop(w, kind, h, axis, to).start()

    def prefix(w, h):
        receive(w, 0, h)
        wire_out[w, 0, h] = (scaled(wire_in[w, 0, h], 2, h) + runs[w][h]).astype(BF16)
        send(w, 0, h)

    def rest(w, h):
        receive(w, 1, h)
        wire_out[w, 1, h] = (
            scaled(runs[w][h], 1 - w, h) + wire_in[w, 1, h].astype(F32)
        ).astype(BF16)
        send(w, 1, h)

    def slot(t, carry):
        @pl.when(t < held)
        def _():
            for a in range(4):
                own_copy(t, a).wait()
                for off in range(1, groups):
                    in_copy(off, t, a).wait_recv()
            gather_states(t)

        @pl.when(t == 0)
        def _():
            for copy in decays:
                copy.wait()
            before = jnp.ones((held, 8, span), F32)
            later = jnp.ones((held, 8, span), F32)
            for b in range(n_o):
                piece = block_decay[b]
                before = before * jnp.where(b < o, piece, 1.0)
                later = later * jnp.where(b > o, piece, 1.0)
            derived[0] = before
            derived[1] = later
            derived[2] = block_decay[o]
            derived[3] = before * later * block_decay[o]

        rising = t - o
        falling = t - (n_o - 1 - o)

        @pl.when(jnp.logical_and(rising >= 0, rising < held))
        def _():
            prefix(0, rising)
            rest(1, rising)

        @pl.when(jnp.logical_and(falling >= 0, falling < held))
        def _():
            prefix(1, falling)
            rest(0, falling)

        @pl.when(t >= n_o - 1)
        def _():
            within(t - (n_o - 1))

        return carry

    lax.fori_loop(0, held + n_o - 1, slot, 0)

    def entering(w):
        def one(h, carry):
            group = scaled(scaled(wire_in[w, 0, h], 2, h), 1 - w, h)
            group += wire_out[w, 1, h].astype(F32)
            receive(w, 2, h)
            wire_out[w, 2, h] = (scaled(wire_in[w, 2, h], 3, h) + group).astype(BF16)
            send(w, 2, h)
            enters[w][h] = scaled(wire_in[w, 2, h], w, h) + wire_in[w, 0, h].astype(F32)
            return carry

        lax.fori_loop(0, held, one, 0)

    early = 2 * i < n_i

    @pl.when(early)
    def _():
        entering(0)
        entering(1)

    @pl.when(jnp.logical_not(early))
    def _():
        entering(1)
        entering(0)

    def leaving(step, a):
        to = lax.rem(me + 1 + step, groups)
        lanes = pl.ds(pl.multiple_of(me * width, width), width)
        return pltpu.make_async_remote_copy(
            src_ref=outs.at[a, to],
            dst_ref=outputs[a].at[:, lanes],
            send_sem=out_send.at[step, a],
            recv_sem=out_recv.at[step, a],
            device_id={"mem": to},
            device_id_type=MESH,
        )

    def finish(step, carry):
        c = lax.rem(me + 1 + step, groups)
        for h in range(held):
            col = cols[c, h]
            past, future = (
                jnp.concatenate(
                    [
                        (
                            local[c, h, :, block(e)]
                            + enter[h, :, block(e)] * near[c, h, e : e + 1, :]
                        ).astype(BF16)
                        for e in range(count)
                    ],
                    1,
                )
                for local, enter, near in (
                    (local_f, enter_f, near_f),
                    (local_b, enter_b, near_b),
                )
            )
            out = part[0, c, h] + dot(qas[c, h], past, 1, 1)
            grad_v = part[3, c, h] + dot(kbs[c, h], future, 1, 1)
            grad_q = part[1, c, h]
            grad_k = part[2, c, h]
            from_past = dot(x[3, h, c], past, 1, 0)
            from_future = dot(x[2, h, c], future, 1, 0)
            for e in range(count):
                grad_q += from_past[:, block(e)] * col[:, count + e : count + e + 1]
                grad_k += from_future[:, block(e)] * col[:, 2 * count + e : 2 * count + e + 1]
            for a, value in enumerate((out, grad_q, grad_k, grad_v)):
                outs[a, c, :, block(h)] = value.astype(BF16)

        @pl.when(step < groups - 1)
        def _():
            for a in range(4):
                leaving(step, a).start()

        return carry

    lax.fori_loop(0, groups, finish, 0)
    lanes = pl.ds(pl.multiple_of(me * width, width), width)
    own = []
    for a in range(4):
        copy = pltpu.make_async_copy(outs.at[a, me], outputs[a].at[:, lanes], own_sem.at[0, a])
        copy.start()
        own.append(copy)
    for copy in own:
        copy.wait()

    def drain(h, carry):
        for a in range(4):
            for off in range(1, groups):
                in_copy(off, h, a).wait_send()
        for (w, kind), (axis, _, allowed, to) in links.items():

            @pl.when(allowed)
            def _():
                hop(w, kind, h, axis, to).wait_send()

        return carry

    lax.fori_loop(0, held, drain, 0)
    for step in range(groups - 1):
        for a in range(4):
            leaving(step, a).wait()


def body(queries, keys, values, log_decay, routes, route_logits, cotangent):
    groups = lax.axis_size("mem")
    n_i = lax.axis_size("seqi")
    n_o = lax.axis_size("seqo")
    memories = MEM_DEV * groups
    span, features = queries.shape[1:]
    heads = log_decay.shape[0]
    held = heads // groups
    count = memories + 1
    scale = 2.0 / math.sqrt(DK * span * groups * n_i * n_o)
    rows = tables(
        log_decay[:, 0, :].astype(F32),
        routes[0],
        route_logits[0].astype(F32),
        groups,
        memories,
        scale,
    )
    any_spec = pl.BlockSpec(memory_space=pl.ANY)
    state = (held, DK, count * DK)
    result = jax.ShapeDtypeStruct((span, features), BF16)
    dma = pltpu.SemaphoreType.DMA
    results = pl.pallas_call(
        functools.partial(kernel, groups, n_i, n_o, held, count),
        out_shape=[result] * 4,
        in_specs=[any_spec] * 5,
        out_specs=[any_spec] * 4,
        scratch_shapes=[
            pltpu.VMEM((4, held, groups, span, DK), BF16),
            pltpu.VMEM((groups, held, 32, span), F32),
            pltpu.VMEM((groups, held, span, 16), F32),
            pltpu.VMEM((4, groups, span, held * DK), BF16),
            pltpu.VMEM((4, groups, held, span, DK), F32),
            pltpu.VMEM((groups, held, span, count * DK), BF16),
            pltpu.VMEM((groups, held, span, count * DK), BF16),
            pltpu.VMEM((groups,) + state, F32),
            pltpu.VMEM((groups,) + state, F32),
            pltpu.VMEM(state, F32),
            pltpu.VMEM(state, F32),
            pltpu.VMEM(state, F32),
            pltpu.VMEM(state, F32),
            pltpu.VMEM((groups, held, 8, span), F32),
            pltpu.VMEM((groups, held, 8, span), F32),
            pltpu.VMEM((n_o, held, 8, span), F32),
            pltpu.VMEM((4, held, 8, span), F32),
            pltpu.VMEM((2, 3) + state, BF16),
            pltpu.VMEM((2, 3) + state, BF16),
            dma((groups - 1,)),
            dma((groups - 1,)),
            dma((groups - 1, held, 4)),
            dma((groups - 1, held, 4)),
            dma((n_o - 1,)),
            dma((n_o - 1,)),
            dma((2, 3, held)),
            dma((2, 3, held)),
            dma((groups - 1, 4)),
            dma((groups - 1, 4)),
            dma,
            dma((held, 4)),
        ],
        compiler_params=pltpu.CompilerParams(
            collective_id=0, has_side_effects=True, vmem_limit_bytes=56 * 1024 * 1024
        ),
        cost_estimate=pl.CostEstimate(
            flops=2 * 36 * heads * DK * DK * span,
            bytes_accessed=16 * span * features,
            transcendentals=0,
        ),
    )(queries[0], keys[0], values[0], cotangent[0], rows)
    return tuple(item[None] for item in results)


def solution(mesh):
    rows = P(("seqi", "seqo"), "mem", None)
    return jax.shard_map(
        body,
        mesh=mesh,
        in_specs=(rows, rows, rows, P(None, ("seqi", "seqo"), "mem"), rows, rows, rows),
        out_specs=(rows, rows, rows, rows),
        check_vma=False,
    )
```

```python
import functools
import math

import jax
import jax.numpy as jnp
from jax import lax
from jax.experimental import pallas as pl
from jax.experimental.pallas import tpu as pltpu
from jax.sharding import PartitionSpec as P

DK = 128
MEM_DEV = 1
MESH = pl.DeviceIdType.MESH
F32 = jnp.float32
BF16 = jnp.bfloat16


def dot(left, right, left_dim, right_dim):
    return lax.dot_general(
        left, right, (((left_dim,), (right_dim,)), ((), ())), preferred_element_type=F32
    )


def tables(gates, chosen, logits, groups, memories, scale):
    heads, span = gates.shape
    held = heads // groups
    first = jax.nn.sigmoid(logits[:, 0] - logits[:, 1]).astype(BF16).astype(F32)
    second = jax.nn.sigmoid(logits[:, 1] - logits[:, 0]).astype(BF16).astype(F32)
    names = jnp.arange(memories, dtype=jnp.int32)[:, None]
    hit_first = (chosen[:, 0][None, :] == names).astype(F32)
    hit_second = (chosen[:, 1][None, :] == names).astype(F32)
    ones = jnp.ones((1, span), F32)
    mask = jnp.concatenate([hit_first + hit_second, ones], 0)
    read = jnp.concatenate([first[None] * hit_first + second[None] * hit_second, ones], 0) * scale
    rates = gates[:, None, :] * mask[None]
    upper = (jnp.arange(span)[:, None] <= jnp.arange(span)[None, :]).astype(F32)
    total = jnp.einsum("het,ts->hes", rates, upper, precision=lax.Precision.HIGHEST)
    middle = total[:, :, span // 2 : span // 2 + 1]
    end = total[:, :, -1:]
    count = memories + 1
    kinds = jnp.concatenate(
        [
            read[None] * jnp.exp(total - middle),
            read[None] * jnp.exp(total),
            mask[None] * jnp.exp(end - total),
            jnp.zeros((heads, 16 - 3 * count, span), F32),
            mask[None] * jnp.exp(middle - total),
            jnp.zeros((heads, 8 - count, span), F32),
            jnp.broadcast_to(jnp.exp(end), total.shape),
            jnp.zeros((heads, 8 - count, span), F32),
        ],
        1,
    )
    return kinds.reshape(groups, held, 32, span)


def kernel(
    groups,
    n_i,
    n_o,
    held,
    count,
    q_ref,
    k_ref,
    v_ref,
    g_ref,
    row_ref,
    out_ref,
    x,
    rows,
    cols,
    outs,
    part,
    kbs,
    qas,
    local_f,
    local_b,
    run_f,
    run_b,
    enter_f,
    enter_b,
    near_f,
    near_b,
    block_decay,
    derived,
    wire_out,
    wire_in,
    row_send,
    row_recv,
    in_send,
    in_recv,
    dec_send,
    dec_recv,
    wire_send,
    wire_recv,
    out_send,
    out_recv,
    row_sem,
    own_sem,
    stay_sem,
):
    span = x.shape[3]
    me = lax.axis_index("mem")
    i = lax.axis_index("seqi")
    o = lax.axis_index("seqo")
    inputs = (q_ref, k_ref, v_ref, g_ref)

    barrier = pltpu.get_barrier_semaphore()
    for off in range(1, groups):
        pl.semaphore_signal(
            barrier, inc=1, device_id={"mem": lax.rem(me + off, groups)}, device_id_type=MESH
        )
    for off in range(1, n_o):
        pl.semaphore_signal(
            barrier, inc=1, device_id={"seqo": lax.rem(o + off, n_o)}, device_id_type=MESH
        )

    @pl.when(i > 0)
    def _():
        pl.semaphore_signal(
            barrier, inc=1, device_id={"seqi": lax.rem(i + n_i - 1, n_i)}, device_id_type=MESH
        )

    @pl.when(i < n_i - 1)
    def _():
        pl.semaphore_signal(
            barrier, inc=1, device_id={"seqi": lax.rem(i + 1, n_i)}, device_id_type=MESH
        )

    sides = jnp.where(i > 0, 1, 0) + jnp.where(i < n_i - 1, 1, 0)
    pl.semaphore_wait(barrier, groups - 1 + n_o - 1 + sides)

    def row_copy(off):
        to = lax.rem(me + off, groups)
        return pltpu.make_async_remote_copy(
            src_ref=row_ref.at[to],
            dst_ref=rows.at[me],
            send_sem=row_send.at[off - 1],
            recv_sem=row_recv.at[off - 1],
            device_id={"mem": to},
            device_id_type=MESH,
        )

    def in_copy(off, h, a):
        to = lax.rem(me + off, groups)
        lanes = pl.ds(pl.multiple_of((to * held + h) * DK, DK), DK)
        return pltpu.make_async_remote_copy(
            src_ref=inputs[a].at[:, lanes],
            dst_ref=x.at[a, h, me],
            send_sem=in_send.at[off - 1, h, a],
            recv_sem=in_recv.at[off - 1, h, a],
            device_id={"mem": to},
            device_id_type=MESH,
        )

    def own_copy(h, a):
        lanes = pl.ds(pl.multiple_of((me * held + h) * DK, DK), DK)
        return pltpu.make_async_copy(inputs[a].at[:, lanes], x.at[a, h, me], own_sem.at[h, a])

    for off in range(1, groups):
        row_copy(off).start()
    own_rows = pltpu.make_async_copy(row_ref.at[me], rows.at[me], row_sem)
    own_rows.start()

    def start_in(h, carry):
        for a in range(4):
            for off in range(1, groups):
                in_copy(off, h, a).start()
            own_copy(h, a).start()
        return carry

    lax.fori_loop(0, held, start_in, 0)
    own_rows.wait()
    for off in range(1, groups):
        row_copy(off).wait()

    chunk_decay = [rows[c, :, 24:32, :] for c in range(groups)]
    total = jnp.ones((held, 8, span), F32)
    for c in range(groups):
        near_f[c] = total
        total = total * chunk_decay[c]
    block_decay[o] = total
    after = jnp.ones((held, 8, span), F32)
    for c in reversed(range(groups)):
        near_b[c] = after
        after = after * chunk_decay[c]
    decays = []
    for off in range(1, n_o):
        copy = pltpu.make_async_remote_copy(
            src_ref=block_decay.at[o],
            dst_ref=block_decay.at[o],
            send_sem=dec_send.at[off - 1],
            recv_sem=dec_recv.at[off - 1],
            device_id={"seqo": lax.rem(o + off, n_o)},
            device_id_type=MESH,
        )
        copy.start()
        decays.append(copy)

    def block(e):
        return slice(e * DK, (e + 1) * DK)

    def gather_states(h):
        run_f[h] = jnp.zeros((DK, count * DK), F32)
        run_b[h] = jnp.zeros((DK, count * DK), F32)
        for c in range(groups):
            col = rows[c, h, 0:16, :].T
            cols[c, h] = col
            for a, saved, first in ((1, kbs, 2 * count), (0, qas, count)):
                value = x[a, h, c].astype(F32)
                saved[c, h] = jnp.concatenate(
                    [
                        (value * col[:, first + e : first + e + 1]).astype(BF16)
                        for e in range(count)
                    ],
                    1,
                )
        for step in range(groups):
            for c, a, saved, run, local in (
                (step, 2, kbs, run_f, local_f),
                (groups - 1 - step, 3, qas, run_b, local_b),
            ):
                state = dot(x[a, h, c], saved[c, h], 0, 0)
                for e in range(count):
                    old = run[h, :, block(e)]
                    local[c, h, :, block(e)] = old
                    run[h, :, block(e)] = old * rows[c, h, 24 + e : 25 + e, :] + state[:, block(e)]

    lower = lax.broadcasted_iota(jnp.int32, (span, span), 0) >= lax.broadcasted_iota(
        jnp.int32, (span, span), 1
    )

    def within(h):
        for c in range(groups):
            q, k, v, g = (x[a, h, c] for a in range(4))
            col = cols[c, h]
            weight = jnp.zeros((span, span), F32)
            for e in range(count):
                weight += col[:, e : e + 1] * rows[c, h, 16 + e : 17 + e, :]
            weight = jnp.where(lower, weight, 0.0)
            sw = (dot(q, k, 1, 1) * weight).astype(BF16)
            gw = (dot(g, v, 1, 1) * weight).astype(BF16)
            part[0, c, h] = dot(sw, v, 1, 0)
            part[1, c, h] = dot(gw, k, 1, 0)
            part[2, c, h] = dot(gw, q, 0, 0)
            part[3, c, h] = dot(sw, g, 0, 0)

    def scaled(value, kind, h):
        return jnp.concatenate(
            [
                value[:, block(e)].astype(F32) * derived[kind, h, e : e + 1, :]
                for e in range(count)
            ],
            1,
        )

    def hop(w, kind, h, axis, to):
        return pltpu.make_async_remote_copy(
            src_ref=wire_out.at[w, kind, h],
            dst_ref=wire_in.at[w, kind, h],
            send_sem=wire_send.at[w, kind, h],
            recv_sem=wire_recv.at[w, kind, h],
            device_id={axis: to},
            device_id_type=MESH,
        )

    up, down = lax.rem(o + 1, n_o), lax.rem(o + n_o - 1, n_o)
    i_up, i_down = lax.rem(i + 1, n_i), lax.rem(i + n_i - 1, n_i)
    low, high = o > 0, o < n_o - 1
    i_low, i_high = i > 0, i < n_i - 1
    runs = (run_f, run_b)
    enters = (enter_f, enter_b)
    along = ((low, high, up), (high, low, down))
    across = ((i_low, i_high, i_up), (i_high, i_low, i_down))
    links = []
    for w in range(2):
        links.append((w, 0, "seqo") + along[w])
        has, to_has, to = along[1 - w]
        passes = across[w][1]
        links.append(
            (w, 1, "seqo", jnp.logical_and(has, passes), jnp.logical_and(to_has, passes), to)
        )
        links.append((w, 2, "seqi") + across[w])
    links = {(w, kind): rest for w, kind, *rest in links}

    def receive(w, kind, h):
        axis, present, _, to = links[w, kind]

        @pl.when(present)
        def _():
            hop(w, kind, h, axis, to).wait_recv()

        @pl.when(jnp.logical_not(present))
        def _():
            wire_in[w, kind, h] = jnp.zeros((DK, count * DK), BF16)

    def send(w, kind, h):
        axis, _, allowed, to = links[w, kind]

        @pl.when(allowed)
        def _():
            hop(w, kind, h, axis, to).start()

    def prefix(w, h):
        receive(w, 0, h)
        wire_out[w, 0, h] = (scaled(wire_in[w, 0, h], 2, h) + runs[w][h]).astype(BF16)
        send(w, 0, h)

    def rest(w, h):
        receive(w, 1, h)
        wire_out[w, 1, h] = (
            scaled(runs[w][h], 1 - w, h) + wire_in[w, 1, h].astype(F32)
        ).astype(BF16)
        send(w, 1, h)

    def slot(t, carry):
        @pl.when(t < held)
        def _():
            for a in range(4):
                own_copy(t, a).wait()
                for off in range(1, groups):
                    in_copy(off, t, a).wait_recv()
            gather_states(t)

        @pl.when(t == 0)
        def _():
            for copy in decays:
                copy.wait()
            before = jnp.ones((held, 8, span), F32)
            later = jnp.ones((held, 8, span), F32)
            for b in range(n_o):
                piece = block_decay[b]
                before = before * jnp.where(b < o, piece, 1.0)
                later = later * jnp.where(b > o, piece, 1.0)
            derived[0] = before
            derived[1] = later
            derived[2] = block_decay[o]
            derived[3] = before * later * block_decay[o]

        rising = t - o
        falling = t - (n_o - 1 - o)

        @pl.when(jnp.logical_and(rising >= 0, rising < held))
        def _():
            prefix(0, rising)
            rest(1, rising)

        @pl.when(jnp.logical_and(falling >= 0, falling < held))
        def _():
            prefix(1, falling)
            rest(0, falling)

        @pl.when(t < held)
        def _():
            within(t)

        for w, place in ((0, i), (1, n_i - 1 - i)):
            crossing = t - (n_o - 1) - place

            @pl.when(jnp.logical_and(crossing >= 0, crossing < held))
            def _():
                entering(w, crossing)

        done = t - (n_o - 1) - (n_i - 1)

        @pl.when(done >= 0)
        def _():
            finish(done)

        return carry

    def entering(w, h):
        group = scaled(scaled(wire_in[w, 0, h], 2, h), 1 - w, h)
        group += wire_out[w, 1, h].astype(F32)
        receive(w, 2, h)
        wire_out[w, 2, h] = (scaled(wire_in[w, 2, h], 3, h) + group).astype(BF16)
        send(w, 2, h)
        enters[w][h] = scaled(wire_in[w, 2, h], w, h) + wire_in[w, 0, h].astype(F32)

    def leaving(step, h, a):
        to = lax.rem(me + 1 + step, groups)
        lanes = pl.ds(pl.multiple_of((me * held + h) * DK, DK), DK)
        return pltpu.make_async_remote_copy(
            src_ref=outs.at[a, h, to],
            dst_ref=out_ref.at[a, :, lanes],
            send_sem=out_send.at[step, h, a],
            recv_sem=out_recv.at[step, h, a],
            device_id={"mem": to},
            device_id_type=MESH,
        )

    def staying(h, a):
        lanes = pl.ds(pl.multiple_of((me * held + h) * DK, DK), DK)
        return pltpu.make_async_copy(outs.at[a, h, me], out_ref.at[a, :, lanes], stay_sem.at[h, a])

    def finish(h):
        for step in range(groups):
            c = lax.rem(me + 1 + step, groups)
            col = cols[c, h]
            past, future = (
                jnp.concatenate(
                    [
                        (
                            local[c, h, :, block(e)]
                            + enter[h, :, block(e)] * near[c, h, e : e + 1, :]
                        ).astype(BF16)
                        for e in range(count)
                    ],
                    1,
                )
                for local, enter, near in (
                    (local_f, enter_f, near_f),
                    (local_b, enter_b, near_b),
                )
            )
            out = part[0, c, h] + dot(qas[c, h], past, 1, 1)
            grad_v = part[3, c, h] + dot(kbs[c, h], future, 1, 1)
            grad_q = part[1, c, h]
            grad_k = part[2, c, h]
            from_past = dot(x[3, h, c], past, 1, 0)
            from_future = dot(x[2, h, c], future, 1, 0)
            for e in range(count):
                grad_q += from_past[:, block(e)] * col[:, count + e : count + e + 1]
                grad_k += from_future[:, block(e)] * col[:, 2 * count + e : 2 * count + e + 1]
            for a, value in enumerate((out, grad_q, grad_k, grad_v)):
                outs[a, h, c] = value.astype(BF16)
            for a in range(4):
                (leaving(step, h, a) if step < groups - 1 else staying(h, a)).start()

    lax.fori_loop(0, held + n_o - 1 + n_i - 1, slot, 0)

    def drain(h, carry):
        for a in range(4):
            for off in range(1, groups):
                in_copy(off, h, a).wait_send()
        for (w, kind), (axis, _, allowed, to) in links.items():

            @pl.when(allowed)
            def _():
                hop(w, kind, h, axis, to).wait_send()

        for a in range(4):
            staying(h, a).wait()
            for step in range(groups - 1):
                leaving(step, h, a).wait()
        return carry

    lax.fori_loop(0, held, drain, 0)


def body(queries, keys, values, log_decay, routes, route_logits, cotangent):
    groups = lax.axis_size("mem")
    n_i = lax.axis_size("seqi")
    n_o = lax.axis_size("seqo")
    memories = MEM_DEV * groups
    span, features = queries.shape[1:]
    heads = log_decay.shape[0]
    held = heads // groups
    count = memories + 1
    scale = 2.0 / math.sqrt(DK * span * groups * n_i * n_o)
    rows = tables(
        log_decay[:, 0, :].astype(F32),
        routes[0],
        route_logits[0].astype(F32),
        groups,
        memories,
        scale,
    )
    any_spec = pl.BlockSpec(memory_space=pl.ANY)
    state = (held, DK, count * DK)
    result = jax.ShapeDtypeStruct((4, span, features), BF16)
    dma = pltpu.SemaphoreType.DMA
    results = pl.pallas_call(
        functools.partial(kernel, groups, n_i, n_o, held, count),
        out_shape=result,
        in_specs=[any_spec] * 5,
        out_specs=any_spec,
        scratch_shapes=[
            pltpu.VMEM((4, held, groups, span, DK), BF16),
            pltpu.VMEM((groups, held, 32, span), F32),
            pltpu.VMEM((groups, held, span, 16), F32),
            pltpu.VMEM((4, held, groups, span, DK), BF16),
            pltpu.VMEM((4, groups, held, span, DK), F32),
            pltpu.VMEM((groups, held, span, count * DK), BF16),
            pltpu.VMEM((groups, held, span, count * DK), BF16),
            pltpu.VMEM((groups,) + state, F32),
            pltpu.VMEM((groups,) + state, F32),
            pltpu.VMEM(state, F32),
            pltpu.VMEM(state, F32),
            pltpu.VMEM(state, F32),
            pltpu.VMEM(state, F32),
            pltpu.VMEM((groups, held, 8, span), F32),
            pltpu.VMEM((groups, held, 8, span), F32),
            pltpu.VMEM((n_o, held, 8, span), F32),
            pltpu.VMEM((4, held, 8, span), F32),
            pltpu.VMEM((2, 3) + state, BF16),
            pltpu.VMEM((2, 3) + state, BF16),
            dma((groups - 1,)),
            dma((groups - 1,)),
            dma((groups - 1, held, 4)),
            dma((groups - 1, held, 4)),
            dma((n_o - 1,)),
            dma((n_o - 1,)),
            dma((2, 3, held)),
            dma((2, 3, held)),
            dma((groups - 1, held, 4)),
            dma((groups - 1, held, 4)),
            dma,
            dma((held, 4)),
            dma((held, 4)),
        ],
        compiler_params=pltpu.CompilerParams(
            collective_id=0, has_side_effects=True, vmem_limit_bytes=56 * 1024 * 1024
        ),
        cost_estimate=pl.CostEstimate(
            flops=2 * 36 * heads * DK * DK * span,
            bytes_accessed=16 * span * features,
            transcendentals=0,
        ),
    )(queries[0], keys[0], values[0], cotangent[0], rows)
    return tuple(results[a : a + 1] for a in range(4))


def solution(mesh):
    rows = P(("seqi", "seqo"), "mem", None)
    return jax.shard_map(
        body,
        mesh=mesh,
        in_specs=(rows, rows, rows, P(None, ("seqi", "seqo"), "mem"), rows, rows, rows),
        out_specs=(rows, rows, rows, rows),
        check_vma=False,
    )
```

```python
import functools
import math

import jax
import jax.numpy as jnp
from jax import lax
from jax.experimental import pallas as pl
from jax.experimental.pallas import tpu as pltpu
from jax.sharding import PartitionSpec as P

DK = 128
MEM_DEV = 1
MESH = pl.DeviceIdType.MESH
F32 = jnp.float32
BF16 = jnp.bfloat16


def dot(left, right, left_dim, right_dim):
    return lax.dot_general(
        left, right, (((left_dim,), (right_dim,)), ((), ())), preferred_element_type=F32
    )


def fill_tables(table, route_ref, logit_ref, gate_ref, scale):
    groups, held, _, span = table.shape
    heads = groups * held
    names = lax.broadcasted_iota(jnp.int32, (8, span), 0)
    logits = logit_ref[...].astype(F32)
    first = jax.nn.sigmoid(logits[0:1] - logits[1:2]).astype(BF16).astype(F32)
    second = jax.nn.sigmoid(logits[1:2] - logits[0:1]).astype(BF16).astype(F32)
    hit_first = (route_ref[0:1, :] == names).astype(F32)
    hit_second = (route_ref[1:2, :] == names).astype(F32)
    shared = (names == MEM_DEV * groups).astype(F32)
    above = lax.broadcasted_iota(jnp.int32, (span, span), 0)
    along = lax.broadcasted_iota(jnp.int32, (span, span), 1)
    upper = (above <= along).astype(F32).astype(BF16)
    mask = hit_first + hit_second + shared
    read = (first * hit_first + second * hit_second + shared) * scale
    gates = gate_ref[...].astype(F32)
    rates = jnp.concatenate([gates[h : h + 1] * mask for h in range(heads)], 0)
    total = dot(rates.astype(BF16), upper, 1, 0)
    middle = total[:, span // 2 : span // 2 + 1]
    end = total[:, span - 1 :]
    masks = jnp.concatenate([mask] * heads, 0)
    reads = jnp.concatenate([read] * heads, 0)
    kinds = (
        reads * jnp.exp(total - middle),
        reads * jnp.exp(total),
        masks * jnp.exp(end - total),
        masks * jnp.exp(middle - total),
        jnp.broadcast_to(jnp.exp(end), total.shape),
    )
    for n, kind in enumerate(kinds):
        table[:, :, 8 * n : 8 * n + 8, :] = kind.reshape(groups, held, 8, span)


def kernel(
    groups,
    n_i,
    n_o,
    held,
    count,
    scale,
    q_ref,
    k_ref,
    v_ref,
    g_ref,
    route_ref,
    logit_ref,
    gate_ref,
    out_ref,
    x,
    row_ref,
    rows,
    cols,
    outs,
    part,
    kbs,
    qas,
    local_f,
    local_b,
    run_f,
    run_b,
    enter_f,
    enter_b,
    near_f,
    near_b,
    block_decay,
    derived,
    wire_out,
    wire_in,
    row_send,
    row_recv,
    in_send,
    in_recv,
    dec_send,
    dec_recv,
    wire_send,
    wire_recv,
    out_send,
    out_recv,
    row_sem,
    own_sem,
    stay_sem,
):
    span = x.shape[3]
    me = lax.axis_index("mem")
    i = lax.axis_index("seqi")
    o = lax.axis_index("seqo")
    inputs = (q_ref, k_ref, v_ref, g_ref)

    barrier = pltpu.get_barrier_semaphore()
    for off in range(1, groups):
        pl.semaphore_signal(
            barrier, inc=1, device_id={"mem": lax.rem(me + off, groups)}, device_id_type=MESH
        )
    for off in range(1, n_o):
        pl.semaphore_signal(
            barrier, inc=1, device_id={"seqo": lax.rem(o + off, n_o)}, device_id_type=MESH
        )

    @pl.when(i > 0)
    def _():
        pl.semaphore_signal(
            barrier, inc=1, device_id={"seqi": lax.rem(i + n_i - 1, n_i)}, device_id_type=MESH
        )

    @pl.when(i < n_i - 1)
    def _():
        pl.semaphore_signal(
            barrier, inc=1, device_id={"seqi": lax.rem(i + 1, n_i)}, device_id_type=MESH
        )

    sides = jnp.where(i > 0, 1, 0) + jnp.where(i < n_i - 1, 1, 0)
    pl.semaphore_wait(barrier, groups - 1 + n_o - 1 + sides)

    def row_copy(off):
        to = lax.rem(me + off, groups)
        return pltpu.make_async_remote_copy(
            src_ref=row_ref.at[to],
            dst_ref=rows.at[me],
            send_sem=row_send.at[off - 1],
            recv_sem=row_recv.at[off - 1],
            device_id={"mem": to},
            device_id_type=MESH,
        )

    def in_copy(off, h, a):
        to = lax.rem(me + off, groups)
        lanes = pl.ds(pl.multiple_of((to * held + h) * DK, DK), DK)
        return pltpu.make_async_remote_copy(
            src_ref=inputs[a].at[:, lanes],
            dst_ref=x.at[a, h, me],
            send_sem=in_send.at[off - 1, h, a],
            recv_sem=in_recv.at[off - 1, h, a],
            device_id={"mem": to},
            device_id_type=MESH,
        )

    def own_copy(h, a):
        lanes = pl.ds(pl.multiple_of((me * held + h) * DK, DK), DK)
        return pltpu.make_async_copy(inputs[a].at[:, lanes], x.at[a, h, me], own_sem.at[h, a])

    def start_in(h, carry):
        for a in range(4):
            for off in range(1, groups):
                in_copy(off, h, a).start()
            own_copy(h, a).start()
        return carry

    start_in(0, 0)
    fill_tables(row_ref, route_ref, logit_ref, gate_ref, scale)
    for off in range(1, groups):
        row_copy(off).start()
    own_rows = pltpu.make_async_copy(row_ref.at[me], rows.at[me], row_sem)
    own_rows.start()
    lax.fori_loop(1, held, start_in, 0)
    for c, local in ((0, local_f), (groups - 1, local_b)):
        local[c] = jnp.zeros((held, DK, count * DK), F32)
    own_rows.wait()
    for off in range(1, groups):
        row_copy(off).wait()

    chunk_decay = [rows[c, :, 32:40, :] for c in range(groups)]
    total = jnp.ones((held, 8, span), F32)
    for c in range(groups):
        near_f[c] = total
        total = total * chunk_decay[c]
    block_decay[o] = total
    after = jnp.ones((held, 8, span), F32)
    for c in reversed(range(groups)):
        near_b[c] = after
        after = after * chunk_decay[c]
    decays = []
    for off in range(1, n_o):
        copy = pltpu.make_async_remote_copy(
            src_ref=block_decay.at[o],
            dst_ref=block_decay.at[o],
            send_sem=dec_send.at[off - 1],
            recv_sem=dec_recv.at[off - 1],
            device_id={"seqo": lax.rem(o + off, n_o)},
            device_id_type=MESH,
        )
        copy.start()
        decays.append(copy)

    def block(e):
        return slice(e * DK, (e + 1) * DK)

    def gather_states(h):
        for c in range(groups):
            col = rows[c, h, 0:24, :].T
            cols[c, h] = col
            for a, saved, first in ((1, kbs, 16), (0, qas, 8)):
                value = x[a, h, c].astype(F32)
                saved[c, h] = jnp.concatenate(
                    [
                        (value * col[:, first + e : first + e + 1]).astype(BF16)
                        for e in range(count)
                    ],
                    1,
                )
        forward = list(range(groups))
        for order, a, saved, run, local in (
            (forward, 2, kbs, run_f, local_f),
            (forward[::-1], 3, qas, run_b, local_b),
        ):
            states = [dot(x[a, h, c], saved[c, h], 0, 0) for c in order]
            for e in range(count):
                total = states[0][:, block(e)]
                for c, state in zip(order[1:], states[1:]):
                    local[c, h, :, block(e)] = total
                    total = total * rows[c, h, 32 + e : 33 + e, :] + state[:, block(e)]
                run[h, :, block(e)] = total

    lower = lax.broadcasted_iota(jnp.int32, (span, span), 0) >= lax.broadcasted_iota(
        jnp.int32, (span, span), 1
    )

    def within(h):
        for c in range(groups):
            q, k, v, g = (x[a, h, c] for a in range(4))
            col = cols[c, h]
            weight = jnp.zeros((span, span), F32)
            for e in range(count):
                weight += col[:, e : e + 1] * rows[c, h, 24 + e : 25 + e, :]
            weight = jnp.where(lower, weight, 0.0)
            sw = (dot(q, k, 1, 1) * weight).astype(BF16)
            gw = (dot(g, v, 1, 1) * weight).astype(BF16)
            part[0, c, h] = dot(sw, v, 1, 0)
            part[1, c, h] = dot(gw, k, 1, 0)
            part[2, c, h] = dot(gw, q, 0, 0)
            part[3, c, h] = dot(sw, g, 0, 0)

    def scaled(value, kind, h):
        return jnp.concatenate(
            [
                value[:, block(e)].astype(F32) * derived[kind, h, e : e + 1, :]
                for e in range(count)
            ],
            1,
        )

    def hop(w, kind, h, axis, to):
        return pltpu.make_async_remote_copy(
            src_ref=wire_out.at[w, kind, h],
            dst_ref=wire_in.at[w, kind, h],
            send_sem=wire_send.at[w, kind, h],
            recv_sem=wire_recv.at[w, kind, h],
            device_id={axis: to},
            device_id_type=MESH,
        )

    up, down = lax.rem(o + 1, n_o), lax.rem(o + n_o - 1, n_o)
    i_up, i_down = lax.rem(i + 1, n_i), lax.rem(i + n_i - 1, n_i)
    low, high = o > 0, o < n_o - 1
    i_low, i_high = i > 0, i < n_i - 1
    runs = (run_f, run_b)
    enters = (enter_f, enter_b)
    along = ((low, high, up), (high, low, down))
    across = ((i_low, i_high, i_up), (i_high, i_low, i_down))
    links = []
    for w in range(2):
        links.append((w, 0, "seqo") + along[w])
        has, to_has, to = along[1 - w]
        passes = across[w][1]
        links.append(
            (w, 1, "seqo", jnp.logical_and(has, passes), jnp.logical_and(to_has, passes), to)
        )
        links.append((w, 2, "seqi") + across[w])
    links = {(w, kind): rest for w, kind, *rest in links}

    def receive(w, kind, h):
        axis, present, _, to = links[w, kind]

        @pl.when(present)
        def _():
            hop(w, kind, h, axis, to).wait_recv()

        @pl.when(jnp.logical_not(present))
        def _():
            wire_in[w, kind, h] = jnp.zeros((DK, count * DK), BF16)

    def send(w, kind, h):
        axis, _, allowed, to = links[w, kind]

        @pl.when(allowed)
        def _():
            hop(w, kind, h, axis, to).start()

    def prefix(w, h):
        receive(w, 0, h)
        wire_out[w, 0, h] = (scaled(wire_in[w, 0, h], 2, h) + runs[w][h]).astype(BF16)
        send(w, 0, h)

    def rest(w, h):
        receive(w, 1, h)
        wire_out[w, 1, h] = (
            scaled(runs[w][h], 1 - w, h) + wire_in[w, 1, h].astype(F32)
        ).astype(BF16)
        send(w, 1, h)

    def slot(t, carry):
        @pl.when(t < held)
        def _():
            for a in range(4):
                own_copy(t, a).wait()
                for off in range(1, groups):
                    in_copy(off, t, a).wait_recv()
            gather_states(t)

        @pl.when(t == 0)
        def _():
            for copy in decays:
                copy.wait()
            before = jnp.ones((held, 8, span), F32)
            later = jnp.ones((held, 8, span), F32)
            for b in range(n_o):
                piece = block_decay[b]
                before = before * jnp.where(b < o, piece, 1.0)
                later = later * jnp.where(b > o, piece, 1.0)
            derived[0] = before
            derived[1] = later
            derived[2] = block_decay[o]
            derived[3] = before * later * block_decay[o]

        rising = t - o
        falling = t - (n_o - 1 - o)

        @pl.when(jnp.logical_and(rising >= 0, rising < held))
        def _():
            prefix(0, rising)
            rest(1, rising)

        @pl.when(jnp.logical_and(falling >= 0, falling < held))
        def _():
            prefix(1, falling)
            rest(0, falling)

        @pl.when(t < held)
        def _():
            within(t)

        for w, place in ((0, i), (1, n_i - 1 - i)):
            crossing = t - (n_o - 1) - place

            @pl.when(jnp.logical_and(crossing >= 0, crossing < held))
            def _():
                entering(w, crossing)

        done = t - (n_o - 1) - (n_i - 1)

        @pl.when(done >= 0)
        def _():
            finish(done)

        return carry

    def entering(w, h):
        group = scaled(scaled(wire_in[w, 0, h], 2, h), 1 - w, h)
        group += wire_out[w, 1, h].astype(F32)
        receive(w, 2, h)
        wire_out[w, 2, h] = (scaled(wire_in[w, 2, h], 3, h) + group).astype(BF16)
        send(w, 2, h)
        enters[w][h] = scaled(wire_in[w, 2, h], w, h) + wire_in[w, 0, h].astype(F32)

    def leaving(step, h, a):
        to = lax.rem(me + 1 + step, groups)
        lanes = pl.ds(pl.multiple_of((me * held + h) * DK, DK), DK)
        return pltpu.make_async_remote_copy(
            src_ref=outs.at[a, h, to],
            dst_ref=out_ref.at[a, :, lanes],
            send_sem=out_send.at[step, h, a],
            recv_sem=out_recv.at[step, h, a],
            device_id={"mem": to},
            device_id_type=MESH,
        )

    def staying(h, a):
        lanes = pl.ds(pl.multiple_of((me * held + h) * DK, DK), DK)
        return pltpu.make_async_copy(outs.at[a, h, me], out_ref.at[a, :, lanes], stay_sem.at[h, a])

    def finish(h):
        for step in range(groups):
            c = lax.rem(me + 1 + step, groups)
            col = cols[c, h]
            past, future = (
                jnp.concatenate(
                    [
                        (
                            local[c, h, :, block(e)]
                            + enter[h, :, block(e)] * near[c, h, e : e + 1, :]
                        ).astype(BF16)
                        for e in range(count)
                    ],
                    1,
                )
                for local, enter, near in (
                    (local_f, enter_f, near_f),
                    (local_b, enter_b, near_b),
                )
            )
            out = part[0, c, h] + dot(qas[c, h], past, 1, 1)
            grad_v = part[3, c, h] + dot(kbs[c, h], future, 1, 1)
            grad_q = part[1, c, h]
            grad_k = part[2, c, h]
            from_past = dot(x[3, h, c], past, 1, 0)
            from_future = dot(x[2, h, c], future, 1, 0)
            for e in range(count):
                grad_q += from_past[:, block(e)] * col[:, 8 + e : 9 + e]
                grad_k += from_future[:, block(e)] * col[:, 16 + e : 17 + e]
            for a, value in enumerate((out, grad_q, grad_k, grad_v)):
                outs[a, h, c] = value.astype(BF16)
            if step % 2 == 1 or step == groups - 1:
                for one in range(step - step % 2, step + 1):
                    for a in range(4):
                        (leaving(one, h, a) if one < groups - 1 else staying(h, a)).start()

    lax.fori_loop(0, held + n_o - 1 + n_i - 1, slot, 0)

    def drain(h, carry):
        for a in range(4):
            for off in range(1, groups):
                in_copy(off, h, a).wait_send()
        for (w, kind), (axis, _, allowed, to) in links.items():

            @pl.when(allowed)
            def _():
                hop(w, kind, h, axis, to).wait_send()

        for a in range(4):
            staying(h, a).wait()
            for step in range(groups - 1):
                leaving(step, h, a).wait()
        return carry

    lax.fori_loop(0, held, drain, 0)


def body(queries, keys, values, log_decay, routes, route_logits, cotangent):
    groups = lax.axis_size("mem")
    n_i = lax.axis_size("seqi")
    n_o = lax.axis_size("seqo")
    memories = MEM_DEV * groups
    span, features = queries.shape[1:]
    heads = log_decay.shape[0]
    held = heads // groups
    count = memories + 1
    scale = 2.0 / math.sqrt(DK * span * groups * n_i * n_o)
    any_spec = pl.BlockSpec(memory_space=pl.ANY)
    state = (held, DK, count * DK)
    result = jax.ShapeDtypeStruct((4, span, features), BF16)
    dma = pltpu.SemaphoreType.DMA
    results = pl.pallas_call(
        functools.partial(kernel, groups, n_i, n_o, held, count, scale),
        out_shape=result,
        in_specs=[any_spec] * 4 + [pl.BlockSpec(memory_space=pltpu.VMEM)] * 3,
        out_specs=any_spec,
        scratch_shapes=[
            pltpu.VMEM((4, held, groups, span, DK), BF16),
            pltpu.VMEM((groups, held, 40, span), F32),
            pltpu.VMEM((groups, held, 40, span), F32),
            pltpu.VMEM((groups, held, span, 24), F32),
            pltpu.VMEM((4, held, groups, span, DK), BF16),
            pltpu.VMEM((4, groups, held, span, DK), F32),
            pltpu.VMEM((groups, held, span, count * DK), BF16),
            pltpu.VMEM((groups, held, span, count * DK), BF16),
            pltpu.VMEM((groups,) + state, F32),
            pltpu.VMEM((groups,) + state, F32),
            pltpu.VMEM(state, F32),
            pltpu.VMEM(state, F32),
            pltpu.VMEM(state, F32),
            pltpu.VMEM(state, F32),
            pltpu.VMEM((groups, held, 8, span), F32),
            pltpu.VMEM((groups, held, 8, span), F32),
            pltpu.VMEM((n_o, held, 8, span), F32),
            pltpu.VMEM((4, held, 8, span), F32),
            pltpu.VMEM((2, 3) + state, BF16),
            pltpu.VMEM((2, 3) + state, BF16),
            dma((groups - 1,)),
            dma((groups - 1,)),
            dma((groups - 1, held, 4)),
            dma((groups - 1, held, 4)),
            dma((n_o - 1,)),
            dma((n_o - 1,)),
            dma((2, 3, held)),
            dma((2, 3, held)),
            dma((groups - 1, held, 4)),
            dma((groups - 1, held, 4)),
            dma,
            dma((held, 4)),
            dma((held, 4)),
        ],
        compiler_params=pltpu.CompilerParams(
            collective_id=0, has_side_effects=True, vmem_limit_bytes=56 * 1024 * 1024
        ),
        cost_estimate=pl.CostEstimate(
            flops=2 * 36 * heads * DK * DK * span,
            bytes_accessed=16 * span * features,
            transcendentals=0,
        ),
    )(queries[0], keys[0], values[0], cotangent[0], routes[0].T, route_logits[0].T, log_decay[:, 0])
    return tuple(results[a : a + 1] for a in range(4))


def solution(mesh):
    rows = P(("seqi", "seqo"), "mem", None)
    return jax.shard_map(
        body,
        mesh=mesh,
        in_specs=(rows, rows, rows, P(None, ("seqi", "seqo"), "mem"), rows, rows, rows),
        out_specs=(rows, rows, rows, rows),
        check_vma=False,
    )
```

```python
import functools
import math

import jax
import jax.numpy as jnp
from jax import lax
from jax.experimental import pallas as pl
from jax.experimental.pallas import tpu as pltpu
from jax.sharding import PartitionSpec as P

DK = 128
MEM_DEV = 1
STRIDE = 2
MESH = pl.DeviceIdType.MESH
F32 = jnp.float32
BF16 = jnp.bfloat16


def dot(left, right, left_dim, right_dim):
    return lax.dot_general(
        left, right, (((left_dim,), (right_dim,)), ((), ())), preferred_element_type=F32
    )


def fill_tables(table, route_ref, logit_ref, gate_ref, scale):
    groups, held, _, span = table.shape
    heads = groups * held
    names = lax.broadcasted_iota(jnp.int32, (8, span), 0)
    logits = logit_ref[...].astype(F32)
    first = jax.nn.sigmoid(logits[0:1] - logits[1:2]).astype(BF16).astype(F32)
    second = jax.nn.sigmoid(logits[1:2] - logits[0:1]).astype(BF16).astype(F32)
    hit_first = (route_ref[0:1, :] == names).astype(F32)
    hit_second = (route_ref[1:2, :] == names).astype(F32)
    shared = (names == MEM_DEV * groups).astype(F32)
    above = lax.broadcasted_iota(jnp.int32, (span, span), 0)
    along = lax.broadcasted_iota(jnp.int32, (span, span), 1)
    upper = (above <= along).astype(F32).astype(BF16)
    mask = hit_first + hit_second + shared
    read = (first * hit_first + second * hit_second + shared) * scale
    gates = gate_ref[...].astype(F32)
    rates = jnp.concatenate([gates[h : h + 1] * mask for h in range(heads)], 0)
    total = dot(rates.astype(BF16), upper, 1, 0)
    middle = total[:, span // 2 : span // 2 + 1]
    end = total[:, span - 1 :]
    masks = jnp.concatenate([mask] * heads, 0)
    reads = jnp.concatenate([read] * heads, 0)
    kinds = (
        reads * jnp.exp(total - middle),
        reads * jnp.exp(total),
        masks * jnp.exp(end - total),
        masks * jnp.exp(middle - total),
        jnp.broadcast_to(jnp.exp(end), total.shape),
    )
    for n, kind in enumerate(kinds):
        table[:, :, 8 * n : 8 * n + 8, :] = kind.reshape(groups, held, 8, span)


def kernel(
    groups,
    n_i,
    n_o,
    held,
    count,
    scale,
    q_ref,
    k_ref,
    v_ref,
    g_ref,
    route_ref,
    logit_ref,
    gate_ref,
    out_ref,
    x,
    row_ref,
    rows,
    cols,
    outs,
    part,
    kbs,
    qas,
    local_f,
    local_b,
    run_f,
    run_b,
    enter_f,
    enter_b,
    near_f,
    near_b,
    block_decay,
    derived,
    wire_out,
    wire_in,
    row_send,
    row_recv,
    in_send,
    in_recv,
    dec_send,
    dec_recv,
    wire_send,
    wire_recv,
    out_send,
    out_recv,
    row_sem,
    own_sem,
    stay_sem,
):
    span = x.shape[3]
    me = lax.axis_index("mem")
    i = lax.axis_index("seqi")
    o = lax.axis_index("seqo")
    inputs = (q_ref, k_ref, v_ref, g_ref)

    barrier = pltpu.get_barrier_semaphore()
    for off in range(1, groups):
        pl.semaphore_signal(
            barrier, inc=1, device_id={"mem": lax.rem(me + off, groups)}, device_id_type=MESH
        )
    for off in range(1, n_o):
        pl.semaphore_signal(
            barrier, inc=1, device_id={"seqo": lax.rem(o + off, n_o)}, device_id_type=MESH
        )

    @pl.when(i > 0)
    def _():
        pl.semaphore_signal(
            barrier, inc=1, device_id={"seqi": lax.rem(i + n_i - 1, n_i)}, device_id_type=MESH
        )

    @pl.when(i < n_i - 1)
    def _():
        pl.semaphore_signal(
            barrier, inc=1, device_id={"seqi": lax.rem(i + 1, n_i)}, device_id_type=MESH
        )

    sides = jnp.where(i > 0, 1, 0) + jnp.where(i < n_i - 1, 1, 0)
    fill_tables(row_ref, route_ref, logit_ref, gate_ref, scale)
    for c, local in ((0, local_f), (groups - 1, local_b)):
        local[c] = jnp.zeros((held, DK, count * DK), F32)
    pl.semaphore_wait(barrier, groups - 1 + n_o - 1 + sides)

    def row_copy(off):
        to = lax.rem(me + off, groups)
        return pltpu.make_async_remote_copy(
            src_ref=row_ref.at[to],
            dst_ref=rows.at[me],
            send_sem=row_send.at[off - 1],
            recv_sem=row_recv.at[off - 1],
            device_id={"mem": to},
            device_id_type=MESH,
        )

    def in_copy(off, h, a):
        to = lax.rem(me + off, groups)
        lanes = pl.ds(pl.multiple_of((to * held + h) * DK, DK), DK)
        return pltpu.make_async_remote_copy(
            src_ref=inputs[a].at[:, lanes],
            dst_ref=x.at[a, h, me],
            send_sem=in_send.at[off - 1, h, a],
            recv_sem=in_recv.at[off - 1, h, a],
            device_id={"mem": to},
            device_id_type=MESH,
        )

    def own_copy(h, a):
        lanes = pl.ds(pl.multiple_of((me * held + h) * DK, DK), DK)
        return pltpu.make_async_copy(inputs[a].at[:, lanes], x.at[a, h, me], own_sem.at[h, a])

    def start_in(h, carry):
        for a in range(4):
            for off in range(1, groups):
                in_copy(off, h, a).start()
            own_copy(h, a).start()
        return carry

    for off in range(1, groups):
        row_copy(off).start()
    own_rows = pltpu.make_async_copy(row_ref.at[me], rows.at[me], row_sem)
    own_rows.start()
    lax.fori_loop(0, held, start_in, 0)
    own_rows.wait()
    for off in range(1, groups):
        row_copy(off).wait()

    chunk_decay = [rows[c, :, 32:40, :] for c in range(groups)]
    total = jnp.ones((held, 8, span), F32)
    for c in range(groups):
        near_f[c] = total
        total = total * chunk_decay[c]
    block_decay[o] = total
    after = jnp.ones((held, 8, span), F32)
    for c in reversed(range(groups)):
        near_b[c] = after
        after = after * chunk_decay[c]
    decays = []
    for off in range(1, n_o):
        copy = pltpu.make_async_remote_copy(
            src_ref=block_decay.at[o],
            dst_ref=block_decay.at[o],
            send_sem=dec_send.at[off - 1],
            recv_sem=dec_recv.at[off - 1],
            device_id={"seqo": lax.rem(o + off, n_o)},
            device_id_type=MESH,
        )
        copy.start()
        decays.append(copy)

    def block(e):
        return slice(e * DK, (e + 1) * DK)

    def gather_states(h):
        for c in range(groups):
            col = rows[c, h, 0:24, :].T
            cols[c, h] = col
            for a, saved, first in ((1, kbs, 16), (0, qas, 8)):
                value = x[a, h, c].astype(F32)
                saved[c, h] = jnp.concatenate(
                    [
                        (value * col[:, first + e : first + e + 1]).astype(BF16)
                        for e in range(count)
                    ],
                    1,
                )
        forward = list(range(groups))
        for order, a, saved, run, local in (
            (forward, 2, kbs, run_f, local_f),
            (forward[::-1], 3, qas, run_b, local_b),
        ):
            states = [dot(x[a, h, c], saved[c, h], 0, 0) for c in order]
            for e in range(count):
                total = states[0][:, block(e)]
                for c, state in zip(order[1:], states[1:]):
                    local[c, h, :, block(e)] = total
                    total = total * rows[c, h, 32 + e : 33 + e, :] + state[:, block(e)]
                run[h, :, block(e)] = total

    lower = lax.broadcasted_iota(jnp.int32, (span, span), 0) >= lax.broadcasted_iota(
        jnp.int32, (span, span), 1
    )

    def within(h):
        for c in range(groups):
            q, k, v, g = (x[a, h, c] for a in range(4))
            col = cols[c, h]
            weight = jnp.zeros((span, span), F32)
            for e in range(count):
                weight += col[:, e : e + 1] * rows[c, h, 24 + e : 25 + e, :]
            weight = jnp.where(lower, weight, 0.0)
            sw = (dot(q, k, 1, 1) * weight).astype(BF16)
            gw = (dot(g, v, 1, 1) * weight).astype(BF16)
            part[0, c, h] = dot(sw, v, 1, 0)
            part[1, c, h] = dot(gw, k, 1, 0)
            part[2, c, h] = dot(gw, q, 0, 0)
            part[3, c, h] = dot(sw, g, 0, 0)

    def scaled(value, kind, h):
        return jnp.concatenate(
            [
                value[:, block(e)].astype(F32) * derived[kind, h, e : e + 1, :]
                for e in range(count)
            ],
            1,
        )

    def hop(w, kind, h, axis, to):
        return pltpu.make_async_remote_copy(
            src_ref=wire_out.at[w, kind, h],
            dst_ref=wire_in.at[w, kind, h],
            send_sem=wire_send.at[w, kind, h],
            recv_sem=wire_recv.at[w, kind, h],
            device_id={axis: to},
            device_id_type=MESH,
        )

    up, down = lax.rem(o + 1, n_o), lax.rem(o + n_o - 1, n_o)
    i_up, i_down = lax.rem(i + 1, n_i), lax.rem(i + n_i - 1, n_i)
    low, high = o > 0, o < n_o - 1
    i_low, i_high = i > 0, i < n_i - 1
    runs = (run_f, run_b)
    enters = (enter_f, enter_b)
    along = ((low, high, up), (high, low, down))
    across = ((i_low, i_high, i_up), (i_high, i_low, i_down))
    links = []
    for w in range(2):
        links.append((w, 0, "seqo") + along[w])
        has, to_has, to = along[1 - w]
        passes = across[w][1]
        links.append(
            (w, 1, "seqo", jnp.logical_and(has, passes), jnp.logical_and(to_has, passes), to)
        )
        links.append((w, 2, "seqi") + across[w])
    links = {(w, kind): rest for w, kind, *rest in links}

    def receive(w, kind, h):
        axis, present, _, to = links[w, kind]

        @pl.when(present)
        def _():
            hop(w, kind, h, axis, to).wait_recv()

        @pl.when(jnp.logical_not(present))
        def _():
            wire_in[w, kind, h] = jnp.zeros((DK, count * DK), BF16)

    def send(w, kind, h):
        axis, _, allowed, to = links[w, kind]

        @pl.when(allowed)
        def _():
            hop(w, kind, h, axis, to).start()

    def prefix(w, h):
        receive(w, 0, h)
        wire_out[w, 0, h] = (scaled(wire_in[w, 0, h], 2, h) + runs[w][h]).astype(BF16)
        send(w, 0, h)

    def rest(w, h):
        receive(w, 1, h)
        wire_out[w, 1, h] = (
            scaled(runs[w][h], 1 - w, h) + wire_in[w, 1, h].astype(F32)
        ).astype(BF16)
        send(w, 1, h)

    def slot(t, carry):
        def step(lag, *work):
            since = t - lag
            h = lax.div(since, STRIDE)
            now = jnp.logical_and(since >= 0, lax.rem(since, STRIDE) == 0)

            @pl.when(jnp.logical_and(now, h < held))
            def _():
                for one in work:
                    one(h)

        def enter_block(h):
            for a in range(4):
                own_copy(h, a).wait()
                for off in range(1, groups):
                    in_copy(off, h, a).wait_recv()
            gather_states(h)

        step(0, enter_block)

        @pl.when(t == 0)
        def _():
            for copy in decays:
                copy.wait()
            before = jnp.ones((held, 8, span), F32)
            later = jnp.ones((held, 8, span), F32)
            for b in range(n_o):
                piece = block_decay[b]
                before = before * jnp.where(b < o, piece, 1.0)
                later = later * jnp.where(b > o, piece, 1.0)
            derived[0] = before
            derived[1] = later
            derived[2] = block_decay[o]
            derived[3] = before * later * block_decay[o]

        step(o, functools.partial(prefix, 0), functools.partial(rest, 1))
        step(n_o - 1 - o, functools.partial(prefix, 1), functools.partial(rest, 0))
        for w, place in ((0, i), (1, n_i - 1 - i)):
            step(n_o - 1 + place, functools.partial(entering, w))
        step(1, within)
        step(n_o - 1 + n_i - 1, finish)
        return carry

    def entering(w, h):
        group = scaled(scaled(wire_in[w, 0, h], 2, h), 1 - w, h)
        group += wire_out[w, 1, h].astype(F32)
        receive(w, 2, h)
        wire_out[w, 2, h] = (scaled(wire_in[w, 2, h], 3, h) + group).astype(BF16)
        send(w, 2, h)
        enters[w][h] = scaled(wire_in[w, 2, h], w, h) + wire_in[w, 0, h].astype(F32)

    def leaving(step, h, a):
        to = lax.rem(me + 1 + step, groups)
        lanes = pl.ds(pl.multiple_of((me * held + h) * DK, DK), DK)
        return pltpu.make_async_remote_copy(
            src_ref=outs.at[a, h, to],
            dst_ref=out_ref.at[a, :, lanes],
            send_sem=out_send.at[step, h, a],
            recv_sem=out_recv.at[step, h, a],
            device_id={"mem": to},
            device_id_type=MESH,
        )

    def staying(h, a):
        lanes = pl.ds(pl.multiple_of((me * held + h) * DK, DK), DK)
        return pltpu.make_async_copy(outs.at[a, h, me], out_ref.at[a, :, lanes], stay_sem.at[h, a])

    def finish(h):
        for step in range(groups):
            c = lax.rem(me + 1 + step, groups)
            col = cols[c, h]
            past, future = (
                jnp.concatenate(
                    [
                        (
                            local[c, h, :, block(e)]
                            + enter[h, :, block(e)] * near[c, h, e : e + 1, :]
                        ).astype(BF16)
                        for e in range(count)
                    ],
                    1,
                )
                for local, enter, near in (
                    (local_f, enter_f, near_f),
                    (local_b, enter_b, near_b),
                )
            )
            out = part[0, c, h] + dot(qas[c, h], past, 1, 1)
            grad_v = part[3, c, h] + dot(kbs[c, h], future, 1, 1)
            grad_q = part[1, c, h]
            grad_k = part[2, c, h]
            from_past = dot(x[3, h, c], past, 1, 0)
            from_future = dot(x[2, h, c], future, 1, 0)
            for e in range(count):
                grad_q += from_past[:, block(e)] * col[:, 8 + e : 9 + e]
                grad_k += from_future[:, block(e)] * col[:, 16 + e : 17 + e]
            for a, value in enumerate((out, grad_q, grad_k, grad_v)):
                outs[a, h, c] = value.astype(BF16)
            if step % 2 == 1 or step == groups - 1:
                for one in range(step - step % 2, step + 1):
                    for a in range(4):
                        (leaving(one, h, a) if one < groups - 1 else staying(h, a)).start()

    lax.fori_loop(0, STRIDE * (held - 1) + n_o + n_i - 1, slot, 0)

    def drain(h, carry):
        for a in range(4):
            for off in range(1, groups):
                in_copy(off, h, a).wait_send()
        for (w, kind), (axis, _, allowed, to) in links.items():

            @pl.when(allowed)
            def _():
                hop(w, kind, h, axis, to).wait_send()

        for a in range(4):
            staying(h, a).wait()
            for step in range(groups - 1):
                leaving(step, h, a).wait()
        return carry

    lax.fori_loop(0, held, drain, 0)


def body(queries, keys, values, log_decay, routes, route_logits, cotangent):
    groups = lax.axis_size("mem")
    n_i = lax.axis_size("seqi")
    n_o = lax.axis_size("seqo")
    memories = MEM_DEV * groups
    span, features = queries.shape[1:]
    heads = log_decay.shape[0]
    held = heads // groups
    count = memories + 1
    scale = 2.0 / math.sqrt(DK * span * groups * n_i * n_o)
    any_spec = pl.BlockSpec(memory_space=pl.ANY)
    state = (held, DK, count * DK)
    result = jax.ShapeDtypeStruct((4, span, features), BF16)
    dma = pltpu.SemaphoreType.DMA
    results = pl.pallas_call(
        functools.partial(kernel, groups, n_i, n_o, held, count, scale),
        out_shape=result,
        in_specs=[any_spec] * 4 + [pl.BlockSpec(memory_space=pltpu.VMEM)] * 3,
        out_specs=any_spec,
        scratch_shapes=[
            pltpu.VMEM((4, held, groups, span, DK), BF16),
            pltpu.VMEM((groups, held, 40, span), F32),
            pltpu.VMEM((groups, held, 40, span), F32),
            pltpu.VMEM((groups, held, span, 24), F32),
            pltpu.VMEM((4, held, groups, span, DK), BF16),
            pltpu.VMEM((4, groups, held, span, DK), F32),
            pltpu.VMEM((groups, held, span, count * DK), BF16),
            pltpu.VMEM((groups, held, span, count * DK), BF16),
            pltpu.VMEM((groups,) + state, F32),
            pltpu.VMEM((groups,) + state, F32),
            pltpu.VMEM(state, F32),
            pltpu.VMEM(state, F32),
            pltpu.VMEM(state, F32),
            pltpu.VMEM(state, F32),
            pltpu.VMEM((groups, held, 8, span), F32),
            pltpu.VMEM((groups, held, 8, span), F32),
            pltpu.VMEM((n_o, held, 8, span), F32),
            pltpu.VMEM((4, held, 8, span), F32),
            pltpu.VMEM((2, 3) + state, BF16),
            pltpu.VMEM((2, 3) + state, BF16),
            dma((groups - 1,)),
            dma((groups - 1,)),
            dma((groups - 1, held, 4)),
            dma((groups - 1, held, 4)),
            dma((n_o - 1,)),
            dma((n_o - 1,)),
            dma((2, 3, held)),
            dma((2, 3, held)),
            dma((groups - 1, held, 4)),
            dma((groups - 1, held, 4)),
            dma,
            dma((held, 4)),
            dma((held, 4)),
        ],
        compiler_params=pltpu.CompilerParams(
            collective_id=0, has_side_effects=True, vmem_limit_bytes=56 * 1024 * 1024
        ),
        cost_estimate=pl.CostEstimate(
            flops=2 * 36 * heads * DK * DK * span,
            bytes_accessed=16 * span * features,
            transcendentals=0,
        ),
    )(queries[0], keys[0], values[0], cotangent[0], routes[0].T, route_logits[0].T, log_decay[:, 0])
    return tuple(results[a : a + 1] for a in range(4))


def solution(mesh):
    rows = P(("seqi", "seqo"), "mem", None)
    return jax.shard_map(
        body,
        mesh=mesh,
        in_specs=(rows, rows, rows, P(None, ("seqi", "seqo"), "mem"), rows, rows, rows),
        out_specs=(rows, rows, rows, rows),
        check_vma=False,
    )
```

```python
import functools
import math

import jax
import jax.numpy as jnp
from jax import lax
from jax.experimental import pallas as pl
from jax.experimental.pallas import tpu as pltpu
from jax.sharding import PartitionSpec as P

DK = 128
MEM_DEV = 1
STRIDE = 1
MESH = pl.DeviceIdType.MESH
F32 = jnp.float32
BF16 = jnp.bfloat16


def dot(left, right, left_dim, right_dim):
    return lax.dot_general(
        left, right, (((left_dim,), (right_dim,)), ((), ())), preferred_element_type=F32
    )


def fill_tables(table, route_ref, logit_ref, gate_ref, scale):
    groups, held, _, span = table.shape
    heads = groups * held
    names = lax.broadcasted_iota(jnp.int32, (8, span), 0)
    logits = logit_ref[...].astype(F32)
    first = jax.nn.sigmoid(logits[0:1] - logits[1:2]).astype(BF16).astype(F32)
    second = jax.nn.sigmoid(logits[1:2] - logits[0:1]).astype(BF16).astype(F32)
    hit_first = (route_ref[0:1, :] == names).astype(F32)
    hit_second = (route_ref[1:2, :] == names).astype(F32)
    shared = (names == MEM_DEV * groups).astype(F32)
    above = lax.broadcasted_iota(jnp.int32, (span, span), 0)
    along = lax.broadcasted_iota(jnp.int32, (span, span), 1)
    upper = (above <= along).astype(F32).astype(BF16)
    mask = hit_first + hit_second + shared
    read = (first * hit_first + second * hit_second + shared) * scale
    gates = gate_ref[...].astype(F32)
    rates = jnp.concatenate([gates[h : h + 1] * mask for h in range(heads)], 0)
    total = dot(rates.astype(BF16), upper, 1, 0)
    middle = total[:, span // 2 : span // 2 + 1]
    end = total[:, span - 1 :]
    masks = jnp.concatenate([mask] * heads, 0)
    reads = jnp.concatenate([read] * heads, 0)
    kinds = (
        reads * jnp.exp(total - middle),
        reads * jnp.exp(total),
        masks * jnp.exp(end - total),
        masks * jnp.exp(middle - total),
        jnp.broadcast_to(jnp.exp(end), total.shape),
    )
    for n, kind in enumerate(kinds):
        table[:, :, 8 * n : 8 * n + 8, :] = kind.reshape(groups, held, 8, span)


def kernel(
    groups,
    n_i,
    n_o,
    held,
    count,
    scale,
    q_ref,
    k_ref,
    v_ref,
    g_ref,
    route_ref,
    logit_ref,
    gate_ref,
    out_ref,
    x,
    row_ref,
    rows,
    cols,
    outs,
    part,
    kbs,
    qas,
    local_f,
    local_b,
    run_f,
    run_b,
    enter_f,
    enter_b,
    near_f,
    near_b,
    block_decay,
    derived,
    wire_out,
    wire_in,
    row_send,
    row_recv,
    in_send,
    in_recv,
    dec_send,
    dec_recv,
    wire_send,
    wire_recv,
    out_send,
    out_recv,
    row_sem,
    own_sem,
    stay_sem,
):
    span = x.shape[3]
    me = lax.axis_index("mem")
    i = lax.axis_index("seqi")
    o = lax.axis_index("seqo")
    inputs = (q_ref, k_ref, v_ref, g_ref)

    barrier = pltpu.get_barrier_semaphore()
    for off in range(1, groups):
        pl.semaphore_signal(
            barrier, inc=1, device_id={"mem": lax.rem(me + off, groups)}, device_id_type=MESH
        )
    for off in range(1, n_o):
        pl.semaphore_signal(
            barrier, inc=1, device_id={"seqo": lax.rem(o + off, n_o)}, device_id_type=MESH
        )

    @pl.when(i > 0)
    def _():
        pl.semaphore_signal(
            barrier, inc=1, device_id={"seqi": lax.rem(i + n_i - 1, n_i)}, device_id_type=MESH
        )

    @pl.when(i < n_i - 1)
    def _():
        pl.semaphore_signal(
            barrier, inc=1, device_id={"seqi": lax.rem(i + 1, n_i)}, device_id_type=MESH
        )

    sides = jnp.where(i > 0, 1, 0) + jnp.where(i < n_i - 1, 1, 0)
    fill_tables(row_ref, route_ref, logit_ref, gate_ref, scale)
    for c, local in ((0, local_f), (groups - 1, local_b)):
        local[c] = jnp.zeros((held, DK, count * DK), F32)
    pl.semaphore_wait(barrier, groups - 1 + n_o - 1 + sides)

    def row_copy(off):
        to = lax.rem(me + off, groups)
        return pltpu.make_async_remote_copy(
            src_ref=row_ref.at[to],
            dst_ref=rows.at[me],
            send_sem=row_send.at[off - 1],
            recv_sem=row_recv.at[off - 1],
            device_id={"mem": to},
            device_id_type=MESH,
        )

    def in_copy(off, h, a):
        to = lax.rem(me + off, groups)
        lanes = pl.ds(pl.multiple_of((to * held + h) * DK, DK), DK)
        return pltpu.make_async_remote_copy(
            src_ref=inputs[a].at[:, lanes],
            dst_ref=x.at[a, h, me],
            send_sem=in_send.at[off - 1, h, a],
            recv_sem=in_recv.at[off - 1, h, a],
            device_id={"mem": to},
            device_id_type=MESH,
        )

    def own_copy(h, a):
        lanes = pl.ds(pl.multiple_of((me * held + h) * DK, DK), DK)
        return pltpu.make_async_copy(inputs[a].at[:, lanes], x.at[a, h, me], own_sem.at[h, a])

    def start_in(h, carry):
        for a in range(4):
            for off in range(1, groups):
                in_copy(off, h, a).start()
            own_copy(h, a).start()
        return carry

    for off in range(1, groups):
        row_copy(off).start()
    own_rows = pltpu.make_async_copy(row_ref.at[me], rows.at[me], row_sem)
    own_rows.start()
    lax.fori_loop(0, held, start_in, 0)
    own_rows.wait()
    for off in range(1, groups):
        row_copy(off).wait()

    chunk_decay = [rows[c, :, 32:40, :] for c in range(groups)]
    total = jnp.ones((held, 8, span), F32)
    for c in range(groups):
        near_f[c] = total
        total = total * chunk_decay[c]
    block_decay[o] = total
    after = jnp.ones((held, 8, span), F32)
    for c in reversed(range(groups)):
        near_b[c] = after
        after = after * chunk_decay[c]
    decays = []
    for off in range(1, n_o):
        copy = pltpu.make_async_remote_copy(
            src_ref=block_decay.at[o],
            dst_ref=block_decay.at[o],
            send_sem=dec_send.at[off - 1],
            recv_sem=dec_recv.at[off - 1],
            device_id={"seqo": lax.rem(o + off, n_o)},
            device_id_type=MESH,
        )
        copy.start()
        decays.append(copy)

    def block(e):
        return slice(e * DK, (e + 1) * DK)

    def gather_states(h):
        for c in range(groups):
            col = rows[c, h, 0:24, :].T
            cols[c, h] = col
            for a, saved, first in ((1, kbs, 16), (0, qas, 8)):
                value = x[a, h, c].astype(F32)
                saved[c, h] = jnp.concatenate(
                    [
                        (value * col[:, first + e : first + e + 1]).astype(BF16)
                        for e in range(count)
                    ],
                    1,
                )
        forward = list(range(groups))
        for order, a, saved, run, local in (
            (forward, 2, kbs, run_f, local_f),
            (forward[::-1], 3, qas, run_b, local_b),
        ):
            states = [dot(x[a, h, c], saved[c, h], 0, 0) for c in order]
            for e in range(count):
                total = states[0][:, block(e)]
                for c, state in zip(order[1:], states[1:]):
                    local[c, h, :, block(e)] = total
                    total = total * rows[c, h, 32 + e : 33 + e, :] + state[:, block(e)]
                run[h, :, block(e)] = total

    lower = lax.broadcasted_iota(jnp.int32, (span, span), 0) >= lax.broadcasted_iota(
        jnp.int32, (span, span), 1
    )

    def within(h):
        for c in range(groups):
            q, k, v, g = (x[a, h, c] for a in range(4))
            col = cols[c, h]
            weight = jnp.zeros((span, span), F32)
            for e in range(count):
                weight += col[:, e : e + 1] * rows[c, h, 24 + e : 25 + e, :]
            weight = jnp.where(lower, weight, 0.0)
            sw = (dot(q, k, 1, 1) * weight).astype(BF16)
            gw = (dot(g, v, 1, 1) * weight).astype(BF16)
            part[0, c, h] = dot(sw, v, 1, 0)
            part[1, c, h] = dot(gw, k, 1, 0)
            part[2, c, h] = dot(gw, q, 0, 0)
            part[3, c, h] = dot(sw, g, 0, 0)

    def scaled(value, kind, h):
        return jnp.concatenate(
            [
                value[:, block(e)].astype(F32) * derived[kind, h, e : e + 1, :]
                for e in range(count)
            ],
            1,
        )

    def hop(w, kind, h, axis, to):
        return pltpu.make_async_remote_copy(
            src_ref=wire_out.at[w, kind, h],
            dst_ref=wire_in.at[w, kind, h],
            send_sem=wire_send.at[w, kind, h],
            recv_sem=wire_recv.at[w, kind, h],
            device_id={axis: to},
            device_id_type=MESH,
        )

    up, down = lax.rem(o + 1, n_o), lax.rem(o + n_o - 1, n_o)
    i_up, i_down = lax.rem(i + 1, n_i), lax.rem(i + n_i - 1, n_i)
    low, high = o > 0, o < n_o - 1
    i_low, i_high = i > 0, i < n_i - 1
    runs = (run_f, run_b)
    enters = (enter_f, enter_b)
    along = ((low, high, up), (high, low, down))
    across = ((i_low, i_high, i_up), (i_high, i_low, i_down))
    links = []
    for w in range(2):
        links.append((w, 0, "seqo") + along[w])
        has, to_has, to = along[1 - w]
        passes = across[w][1]
        links.append(
            (w, 1, "seqo", jnp.logical_and(has, passes), jnp.logical_and(to_has, passes), to)
        )
        links.append((w, 2, "seqi") + across[w])
    links = {(w, kind): rest for w, kind, *rest in links}

    def receive(w, kind, h):
        axis, present, _, to = links[w, kind]

        @pl.when(present)
        def _():
            hop(w, kind, h, axis, to).wait_recv()

        @pl.when(jnp.logical_not(present))
        def _():
            wire_in[w, kind, h] = jnp.zeros((DK, count * DK), BF16)

    def send(w, kind, h):
        axis, _, allowed, to = links[w, kind]

        @pl.when(allowed)
        def _():
            hop(w, kind, h, axis, to).start()

    def prefix(w, h):
        receive(w, 0, h)
        wire_out[w, 0, h] = (scaled(wire_in[w, 0, h], 2, h) + runs[w][h]).astype(BF16)
        send(w, 0, h)

    def rest(w, h):
        receive(w, 1, h)
        wire_out[w, 1, h] = (
            scaled(runs[w][h], 1 - w, h) + wire_in[w, 1, h].astype(F32)
        ).astype(BF16)
        send(w, 1, h)

    def slot(t, carry):
        def step(lag, *work):
            since = t - lag
            h = lax.div(since, STRIDE)
            now = jnp.logical_and(since >= 0, lax.rem(since, STRIDE) == 0)

            @pl.when(jnp.logical_and(now, h < held))
            def _():
                for one in work:
                    one(h)

        def enter_block(h):
            for a in range(4):
                own_copy(h, a).wait()
                for off in range(1, groups):
                    in_copy(off, h, a).wait_recv()
            gather_states(h)

        step(0, enter_block)

        @pl.when(t == 0)
        def _():
            for copy in decays:
                copy.wait()
            before = jnp.ones((held, 8, span), F32)
            later = jnp.ones((held, 8, span), F32)
            for b in range(n_o):
                piece = block_decay[b]
                before = before * jnp.where(b < o, piece, 1.0)
                later = later * jnp.where(b > o, piece, 1.0)
            derived[0] = before
            derived[1] = later
            derived[2] = block_decay[o]
            derived[3] = before * later * block_decay[o]

        step(o, functools.partial(prefix, 0), functools.partial(rest, 1))
        step(n_o - 1 - o, functools.partial(prefix, 1), functools.partial(rest, 0))
        for w, place in ((0, i), (1, n_i - 1 - i)):
            step(n_o - 1 + place, functools.partial(entering, w))
        step(1, within)
        step(n_o - 1 + n_i - 1, finish)
        return carry

    def entering(w, h):
        group = scaled(scaled(wire_in[w, 0, h], 2, h), 1 - w, h)
        group += wire_out[w, 1, h].astype(F32)
        receive(w, 2, h)
        wire_out[w, 2, h] = (scaled(wire_in[w, 2, h], 3, h) + group).astype(BF16)
        send(w, 2, h)
        enters[w][h] = scaled(wire_in[w, 2, h], w, h) + wire_in[w, 0, h].astype(F32)

    def leaving(step, h, a):
        to = lax.rem(me + 1 + step, groups)
        lanes = pl.ds(pl.multiple_of((me * held + h) * DK, DK), DK)
        return pltpu.make_async_remote_copy(
            src_ref=outs.at[a, h, to],
            dst_ref=out_ref.at[a, :, lanes],
            send_sem=out_send.at[step, h, a],
            recv_sem=out_recv.at[step, h, a],
            device_id={"mem": to},
            device_id_type=MESH,
        )

    def staying(h, a):
        lanes = pl.ds(pl.multiple_of((me * held + h) * DK, DK), DK)
        return pltpu.make_async_copy(outs.at[a, h, me], out_ref.at[a, :, lanes], stay_sem.at[h, a])

    def finish(h):
        for step in range(groups):
            c = lax.rem(me + 1 + step, groups)
            col = cols[c, h]
            past, future = (
                jnp.concatenate(
                    [
                        (
                            local[c, h, :, block(e)]
                            + enter[h, :, block(e)] * near[c, h, e : e + 1, :]
                        ).astype(BF16)
                        for e in range(count)
                    ],
                    1,
                )
                for local, enter, near in (
                    (local_f, enter_f, near_f),
                    (local_b, enter_b, near_b),
                )
            )
            out = part[0, c, h] + dot(qas[c, h], past, 1, 1)
            grad_v = part[3, c, h] + dot(kbs[c, h], future, 1, 1)
            grad_q = part[1, c, h]
            grad_k = part[2, c, h]
            from_past = dot(x[3, h, c], past, 1, 0)
            from_future = dot(x[2, h, c], future, 1, 0)
            for e in range(count):
                grad_q += from_past[:, block(e)] * col[:, 8 + e : 9 + e]
                grad_k += from_future[:, block(e)] * col[:, 16 + e : 17 + e]
            for a, value in enumerate((out, grad_q, grad_k, grad_v)):
                outs[a, h, c] = value.astype(BF16)
            if step % 2 == 1 or step == groups - 1:
                for one in range(step - step % 2, step + 1):
                    for a in range(4):
                        (leaving(one, h, a) if one < groups - 1 else staying(h, a)).start()

    lax.fori_loop(0, STRIDE * (held - 1) + n_o + n_i - 1, slot, 0)

    def drain(h, carry):
        for a in range(4):
            for off in range(1, groups):
                in_copy(off, h, a).wait_send()
        for (w, kind), (axis, _, allowed, to) in links.items():

            @pl.when(allowed)
            def _():
                hop(w, kind, h, axis, to).wait_send()

        for a in range(4):
            staying(h, a).wait()
            for step in range(groups - 1):
                leaving(step, h, a).wait()
        return carry

    lax.fori_loop(0, held, drain, 0)


def body(queries, keys, values, log_decay, routes, route_logits, cotangent):
    groups = lax.axis_size("mem")
    n_i = lax.axis_size("seqi")
    n_o = lax.axis_size("seqo")
    memories = MEM_DEV * groups
    span, features = queries.shape[1:]
    heads = log_decay.shape[0]
    held = heads // groups
    count = memories + 1
    scale = 2.0 / math.sqrt(DK * span * groups * n_i * n_o)
    any_spec = pl.BlockSpec(memory_space=pl.ANY)
    state = (held, DK, count * DK)
    result = jax.ShapeDtypeStruct((4, span, features), BF16)
    dma = pltpu.SemaphoreType.DMA
    results = pl.pallas_call(
        functools.partial(kernel, groups, n_i, n_o, held, count, scale),
        out_shape=result,
        in_specs=[any_spec] * 4 + [pl.BlockSpec(memory_space=pltpu.VMEM)] * 3,
        out_specs=any_spec,
        scratch_shapes=[
            pltpu.VMEM((4, held, groups, span, DK), BF16),
            pltpu.VMEM((groups, held, 40, span), F32),
            pltpu.VMEM((groups, held, 40, span), F32),
            pltpu.VMEM((groups, held, span, 24), F32),
            pltpu.VMEM((4, held, groups, span, DK), BF16),
            pltpu.VMEM((4, groups, held, span, DK), F32),
            pltpu.VMEM((groups, held, span, count * DK), BF16),
            pltpu.VMEM((groups, held, span, count * DK), BF16),
            pltpu.VMEM((groups,) + state, F32),
            pltpu.VMEM((groups,) + state, F32),
            pltpu.VMEM(state, F32),
            pltpu.VMEM(state, F32),
            pltpu.VMEM(state, F32),
            pltpu.VMEM(state, F32),
            pltpu.VMEM((groups, held, 8, span), F32),
            pltpu.VMEM((groups, held, 8, span), F32),
            pltpu.VMEM((n_o, held, 8, span), F32),
            pltpu.VMEM((4, held, 8, span), F32),
            pltpu.VMEM((2, 3) + state, BF16),
            pltpu.VMEM((2, 3) + state, BF16),
            dma((groups - 1,)),
            dma((groups - 1,)),
            dma((groups - 1, held, 4)),
            dma((groups - 1, held, 4)),
            dma((n_o - 1,)),
            dma((n_o - 1,)),
            dma((2, 3, held)),
            dma((2, 3, held)),
            dma((groups - 1, held, 4)),
            dma((groups - 1, held, 4)),
            dma,
            dma((held, 4)),
            dma((held, 4)),
        ],
        compiler_params=pltpu.CompilerParams(
            collective_id=0, has_side_effects=True, vmem_limit_bytes=56 * 1024 * 1024
        ),
        cost_estimate=pl.CostEstimate(
            flops=2 * 36 * heads * DK * DK * span,
            bytes_accessed=16 * span * features,
            transcendentals=0,
        ),
    )(queries[0], keys[0], values[0], cotangent[0], routes[0].T, route_logits[0].T, log_decay[:, 0])
    return tuple(results[a : a + 1] for a in range(4))


def solution(mesh):
    rows = P(("seqi", "seqo"), "mem", None)
    return jax.shard_map(
        body,
        mesh=mesh,
        in_specs=(rows, rows, rows, P(None, ("seqi", "seqo"), "mem"), rows, rows, rows),
        out_specs=(rows, rows, rows, rows),
        check_vma=False,
    )
```
